32 devices in a mesh: grow: 8 (over z, x), wide: 4 (over y, core).
Axes of the slice: x: 2, y: 2, z: 4, core: 2. Of those that a mesh axis runs over, the one named last changes fastest.
Arguments:
- fields: float32 [3, 128, 128, 128], P(None, 'grow', 'wide'), may hold values from -1 to 1
- melt_planes: float32 [3, 16, 128, 128], P(None, None, 'wide'), may hold values from -1 to 1
- slide_planes: int32 [8], replicated, may hold values from 0 to 8, as said below
Outputs:
- evolved: float32 [3, 128, 128, 128], P(None, 'grow', 'wide')
The draws below stay inside these ranges and needn't reach their ends.
Inputs may be any that keep to these rules, and one draw needn't show every extreme that they name: `slide_planes`: entries at even positions k are 0; at least one entry equals 8, and at most one other entry is nonzero.
All inputs are finite; a program needn't handle non-finite values.
Results may differ from the reference program's by a relative error of at most 0.0001.
Values sent between devices are 32-bit elements; how exact they have to be, the bound alone decides.
No kernel may reach another device: no remote copies, remote signals or barrier semaphores. Data moves between devices by JAX's collectives and lax.ppermute only.
A program may use at most 64 MiB of HBM per device.

```python
import jax
import jax.numpy as jnp
from jax import lax

CX = 16
NZ = 128
SUBSTEPS = 8
NX = 128
NY = 128


def draw_slide_planes(key, part):
    base = jax.random.fold_in(key, 7)
    key_order, key_count = jax.random.split(base)
    ranking = jax.random.permutation(key_order, SUBSTEPS // 2)
    second_count = jax.random.randint(key_count, (), 0, CX // 2 + 1)
    counts = jnp.where(ranking == 0, CX // 2, jnp.where(ranking == 1, second_count, 0)).astype(jnp.int32)
    odd_slots = 2 * jnp.arange(SUBSTEPS // 2) + 1
    planes = jnp.zeros((SUBSTEPS,), jnp.int32).at[odd_slots].set(counts)
    return planes


def shard_levels(key, shape, cuts, low, high):
    loudness, own = 1.0, jax.random.fold_in(key, 6)
    for dim, parts in cuts:
        steps = jnp.exp(jax.random.uniform(jax.random.fold_in(own, dim), (parts,), jnp.float32, low / len(cuts), high / len(cuts)))
        loudness = loudness * jnp.repeat(steps, shape[dim] // parts).reshape([-1 if axis == dim else 1 for axis in range(len(shape))])
    return loudness


def setup_inputs(seed: int = 0) -> dict:
    key_list = jax.random.split(jax.random.key(seed), 4)
    return {
        "fields": jnp.clip(jax.random.uniform(key_list[0], (3, NX, NY, NZ), jnp.float32, -1.0, 1.0) * shard_levels(key_list[0], (3, NX, NY, NZ), ((1, 8), (2, 4)), -0.4, 0.0), -1.0, 1.0),
        "melt_planes": jnp.clip(jax.random.uniform(key_list[1], (3, CX, NY, NZ), jnp.float32, -1.0, 1.0) * shard_levels(key_list[1], (3, CX, NY, NZ), ((2, 4),), -0.4, 0.0), -1.0, 1.0),
        "slide_planes": draw_slide_planes(jax.random.fold_in(key_list[3], 71), 0),
    }


coef_phase = 0.15
coef_react = 0.3
coef_couple = 0.4
coef_solute = 1.5
coef_diff = 0.1
coef_heat = 0.16


def laplace(field):
    padded = jnp.pad(field, ((1, 1), (1, 1), (0, 0)))
    return (padded[2:, 1:-1] + padded[:-2, 1:-1] + padded[1:-1, 2:] + padded[1:-1, :-2]
            + jnp.roll(field, 1, 2) + jnp.roll(field, -1, 2) - 6.0 * field)


def advance(phase_now, solute, thermal):
    squared = 1.0 - phase_now * phase_now
    driving = (phase_now + coef_phase * laplace(phase_now)
               + coef_react * (phase_now - phase_now * phase_now * phase_now)
               - coef_couple * squared * squared * (thermal + coef_solute * solute))
    grown = jnp.tanh(driving)
    change = 0.5 * (grown - phase_now)
    solute_next = solute + coef_diff * laplace(solute) + change
    thermal_next = thermal + coef_heat * laplace(thermal) + change
    return grown, solute_next, thermal_next


def slide_field(field, melt_field, shift, cursor):
    doubled = jnp.concatenate([melt_field, melt_field], 0)
    entering = lax.dynamic_slice_in_dim(doubled, cursor, CX, 0)
    combined = jnp.concatenate([field, entering], 0)
    return lax.dynamic_slice_in_dim(combined, shift, NX, 0)


def reference(fields, melt_planes, slide_planes):
    phase_now, solute, thermal = fields[0], fields[1], fields[2]
    for substep in range(SUBSTEPS):
        phase_now, solute, thermal = advance(phase_now, solute, thermal)
        shift = slide_planes[substep].astype(jnp.int32)
        cursor = jnp.sum(slide_planes[:substep]).astype(jnp.int32)
        phase_now = slide_field(phase_now, melt_planes[0], shift, cursor)
        solute = slide_field(solute, melt_planes[1], shift, cursor)
        thermal = slide_field(thermal, melt_planes[2], shift, cursor)
    return jnp.stack([phase_now, solute, thermal])
```

```python
import jax
import jax.numpy as jnp
from jax import lax
from jax.experimental import pallas as pl
from jax.experimental.pallas import tpu as pltpu
from jax.sharding import PartitionSpec as P

TILE = 8
GROUP = 6

coef_phase = 0.15
coef_react = 0.3
coef_couple = 0.4
coef_solute = 1.5
coef_diff = 0.1
coef_heat = 0.16


def passed(value, grow_step, wide_pairs=None):
    grow, wide = lax.axis_size("grow"), lax.axis_size("wide")
    if wide_pairs is None:
        return lax.ppermute(value, "grow", [(g, g + grow_step) for g in range(grow) if 0 <= g + grow_step < grow])
    lanes = wide_pairs + [(b, a) for a, b in wide_pairs]
    if grow_step == 0:
        return lax.ppermute(value, "wide", lanes)
    pairs = [
        (g * wide + a, (g + grow_step) * wide + b)
        for g in range(grow)
        if 0 <= g + grow_step < grow
        for a, b in lanes
    ]
    return lax.ppermute(value, ("grow", "wide"), pairs)


def evolve_kernel(slide_ref, own, near, far, melt, outer_own, outer_melt, outer_near, outer_far,
                  inner_own, inner_melt, inner_near, inner_far, out, even, odd, sems, out_sem):
    rows, cols = own.shape[1], own.shape[2]
    steps = slide_ref.shape[0]
    reach = steps
    count = rows + 2 * reach
    zero_slot = count + 2 * reach
    first_col = 2 * TILE
    total_rows = rows * lax.axis_size("grow")
    grow_index, wide_index = lax.axis_index("grow"), lax.axis_index("wide")
    at_end = grow_index == lax.axis_size("grow") - 1
    next_end = grow_index == lax.axis_size("grow") - 2
    is_even = lax.rem(wide_index, 2) == 0
    low_inside = wide_index > 0
    high_inside = wide_index < lax.axis_size("wide") - 1

    total = slide_ref[0]
    for k in range(1, steps):
        total = total + slide_ref[k]
    extra = total - reach
    base = grow_index * rows + extra - reach
    low_col, high_col = first_col - reach, first_col + cols
    outer_col = pl.multiple_of(jnp.where(is_even, low_col, high_col), TILE)
    inner_col = pl.multiple_of(jnp.where(is_even, high_col, low_col), TILE)

    def fetch(source, first, length, col, width, sem):
        return pltpu.make_async_copy(
            source.at[:, pl.ds(0, length)],
            even.at[:, pl.ds(reach - extra + first, length), pl.ds(col, width)],
            sems.at[sem],
        )

    def part(first, length, block, outer, inner, sem):
        return [
            fetch(block, first, length, first_col, cols, sem),
            fetch(outer, first, length, outer_col, reach, sem + 1),
            fetch(inner, first, length, inner_col, reach, sem + 2),
        ]

    near_len, far_len = near.shape[1], far.shape[1]
    own_part = part(0, rows, own, outer_own, inner_own, 0)
    near_part = part(rows, near_len, near, outer_near, inner_near, 3)
    near_melt = part(rows, near_len, melt, outer_melt, inner_melt, 3)
    far_part = part(2 * rows, far_len, far, outer_far, inner_far, 6)
    far_melt = part(2 * rows, far_len, melt, outer_melt, inner_melt, 6)

    def both(act):
        for copy in own_part:
            act(copy)

        @pl.when(at_end)
        def _():
            for copy in near_melt:
                act(copy)

        @pl.when(jnp.logical_not(at_end))
        def _():
            for copy in near_part:
                act(copy)

        @pl.when(next_end)
        def _():
            for copy in far_melt:
                act(copy)

        @pl.when(jnp.logical_not(next_end))
        def _():
            for copy in far_part:
                act(copy)

    both(lambda copy: copy.start())
    for field in range(3):
        for buffer in (even, odd):
            buffer[field, zero_slot] = jnp.zeros_like(buffer[field, zero_slot])
    both(lambda copy: copy.wait())

    tiles = cols // TILE + 2 * (reach // TILE)
    first_row = first_col - reach
    cursor = jnp.int32(0)
    for k in range(steps):
        source, target = (even, odd) if k % 2 == 0 else (odd, even)
        next_cursor = cursor + slide_ref[k]
        top = cursor + total_rows - base
        bottom = next_cursor - base
        last = k == steps - 1
        low, high = reach + k + 1, reach + count - 1 - k
        live_low = jnp.clip(bottom, low, high)
        live_high = jnp.clip(top, live_low, high)

        def group(j, carry):
            r = live_low + GROUP * j
            slots = [r - 1, r] + [jnp.where(r + q < top, r + q, zero_slot) for q in range(1, GROUP + 1)]
            for t in range(1, tiles - 1) if last else range(tiles):
                s0 = first_row + TILE * t
                centre = [[source[f, slot, pl.ds(s0, TILE)] for slot in slots] for f in range(3)]
                for i in range(GROUP):
                    slot = slots[1 + i]
                    value, around = [], []
                    for f in range(3):
                        c = centre[f][1 + i]
                        around.append(
                            (centre[f][i] + centre[f][i + 2])
                            + (source[f, slot, pl.ds(s0 - 1, TILE)] + source[f, slot, pl.ds(s0 + 1, TILE)])
                            + (pltpu.roll(c, 1, 1) + pltpu.roll(c, c.shape[1] - 1, 1))
                        )
                        value.append(c)
                    phase, solute, heat = value
                    squared = phase * phase
                    rest = 1.0 - squared
                    drive = (
                        coef_phase * around[0]
                        + phase * ((1.0 - 6.0 * coef_phase + coef_react) - coef_react * squared)
                        - (rest * rest) * (coef_couple * heat + (coef_couple * coef_solute) * solute)
                    )
                    grown = jnp.tanh(drive)
                    change = 0.5 * (grown - phase)
                    result = [
                        grown,
                        (1.0 - 6.0 * coef_diff) * solute + (coef_diff * around[1] + change),
                        (1.0 - 6.0 * coef_heat) * heat + (coef_heat * around[2] + change),
                    ]
                    if t == 0:
                        result = [jnp.where(low_inside, v, 0.0) for v in result]
                    if t == tiles - 1:
                        result = [jnp.where(high_inside, v, 0.0) for v in result]
                    for f in range(3):
                        target[f, r + i, pl.ds(s0, TILE)] = result[f]
            return carry

        lax.fori_loop(0, (live_high - live_low + GROUP - 1) // GROUP, group, 0)

        def clear(r, carry):
            for f in range(3):
                target[f, r, pl.ds(first_row, TILE * tiles)] = jnp.zeros((TILE * tiles, target.shape[3]), jnp.float32)
            return carry

        def keep(r, carry):
            for f in range(3):
                target[f, r, pl.ds(first_row, TILE * tiles)] = source[f, r, pl.ds(first_row, TILE * tiles)]
            return carry

        lax.fori_loop(low, live_low, clear, 0)
        lax.fori_loop(live_high, high, keep, 0)
        cursor = next_cursor

    final = even if steps % 2 == 0 else odd
    copy = pltpu.make_async_copy(final.at[:, pl.ds(2 * reach, rows), pl.ds(first_col, cols)], out, out_sem)
    copy.start()
    copy.wait()


def evolve(slide_planes, *arrays):
    own = arrays[0]
    rows, cols, depth = own.shape[1:]
    reach = slide_planes.shape[0]
    buffer = pltpu.VMEM((3, rows + 4 * reach + 1, cols + 4 * TILE, depth), jnp.float32)
    anywhere = pl.BlockSpec(memory_space=pl.ANY)
    return pl.pallas_call(
        evolve_kernel,
        out_shape=jax.ShapeDtypeStruct(own.shape, own.dtype),
        in_specs=[pl.BlockSpec(memory_space=pltpu.SMEM)] + [anywhere] * len(arrays),
        out_specs=anywhere,
        scratch_shapes=[buffer, buffer, pltpu.SemaphoreType.DMA((9,)), pltpu.SemaphoreType.DMA],
        compiler_params=pltpu.CompilerParams(vmem_limit_bytes=40 * 1024 * 1024),
    )(slide_planes, *arrays)


def body(fields, melt_planes, slide_planes):
    rows, cols = fields.shape[1], fields.shape[2]
    reach = slide_planes.shape[0]
    wide = lax.axis_size("wide")
    inner_pairs = [(a, a + 1) for a in range(0, wide - 1, 2)]
    outer_pairs = [(a, a + 1) for a in range(1, wide - 1, 2)]
    is_even = lax.rem(lax.axis_index("wide"), 2) == 0
    outer_start = jnp.where(is_even, 0, cols - reach)
    inner_start = jnp.where(is_even, cols - reach, 0)

    def edge(block, start):
        return lax.dynamic_slice_in_dim(block, start, reach, 2)

    near = passed(fields, -1)
    outer = edge(fields, outer_start)
    outer_near = passed(outer, -1, outer_pairs)
    far = passed(fields[:, :reach], -2)
    outer_far = passed(outer[:, :reach], -2, outer_pairs)
    outer_own = passed(outer, 0, outer_pairs)
    outer_melt = passed(edge(melt_planes, outer_start), 0, outer_pairs)
    inner_own = passed(edge(fields, inner_start), 0, inner_pairs)
    inner_melt = passed(edge(melt_planes, inner_start), 0, inner_pairs)
    inner_near = passed(edge(near, inner_start), 0, inner_pairs)
    inner_far = passed(edge(far, inner_start), 0, inner_pairs)
    return evolve(
        slide_planes, fields, near, far, melt_planes,
        outer_own, outer_melt, outer_near, outer_far,
        inner_own, inner_melt, inner_near, inner_far,
    )


def solution(mesh):
    return jax.shard_map(
        body,
        mesh=mesh,
        in_specs=(P(None, "grow", "wide", None), P(None, None, "wide", None), P()),
        out_specs=P(None, "grow", "wide", None),
        check_vma=False,
    )
```

```python
import functools

import jax
import jax.numpy as jnp
from jax import lax
from jax.experimental import pallas as pl
from jax.experimental.pallas import tpu as pltpu
from jax.sharding import PartitionSpec as P

TILE = 8
EARLY, MIDDLE, LATE = 0, 1, 2
GROUPS = (6, 8, 4)
COST = (24000000, 14000000, 7000000)

coef_phase = 0.15
coef_react = 0.3
coef_couple = 0.4
coef_solute = 1.5
coef_diff = 0.1
coef_heat = 0.16


def passed(value, grow_step, wide_pairs=None):
    grow, wide = lax.axis_size("grow"), lax.axis_size("wide")
    if wide_pairs is None:
        return lax.ppermute(value, "grow", [(g, g + grow_step) for g in range(grow) if 0 <= g + grow_step < grow])
    lanes = wide_pairs + [(b, a) for a, b in wide_pairs]
    if grow_step == 0:
        return lax.ppermute(value, "wide", lanes)
    pairs = [
        (g * wide + a, (g + grow_step) * wide + b)
        for g in range(grow)
        if 0 <= g + grow_step < grow
        for a, b in lanes
    ]
    return lax.ppermute(value, ("grow", "wide"), pairs)


def stage_kernel(stage, rows, cols, slide_ref, *refs):
    steps = slide_ref.shape[0]
    reach = steps
    count = rows + 2 * reach
    zero_slot = count + 2 * reach
    first_col = 2 * TILE
    first_row = first_col - reach
    tiles = cols // TILE + 2 * (reach // TILE)
    total_rows = rows * lax.axis_size("grow")
    grow_index, wide_index = lax.axis_index("grow"), lax.axis_index("wide")
    at_end = grow_index == lax.axis_size("grow") - 1
    next_end = grow_index == lax.axis_size("grow") - 2
    is_even = lax.rem(wide_index, 2) == 0
    low_inside = wide_index > 0
    high_inside = wide_index < lax.axis_size("wide") - 1
    group = GROUPS[stage]

    total = slide_ref[0]
    for k in range(1, steps):
        total = total + slide_ref[k]
    extra = total - reach
    base = grow_index * rows + extra - reach
    low_col, high_col = first_row, first_col + cols
    outer_col = pl.multiple_of(jnp.where(is_even, low_col, high_col), TILE)
    inner_col = pl.multiple_of(jnp.where(is_even, high_col, low_col), TILE)

    if stage == EARLY:
        own, outer_both, inner_both, even, odd, token, sems = refs
    elif stage == MIDDLE:
        near, melt, outer_both, inner_both, outer_near, inner_near, _, _, even, odd, token, sems = refs
    else:
        far_low, far_high, inner_far, melt, outer_both, inner_both, _, _, out, even, odd, sems = refs

    def fetch(source, start, col_from, width, length, first, col, sem):
        return pltpu.make_async_copy(
            source.at[:, pl.ds(start, length), pl.ds(col_from, width)],
            even.at[:, pl.ds(reach - extra + first, length), pl.ds(col, width)],
            sems.at[sem],
        )

    def part(first, length, block, outer, inner, sem):
        return [
            fetch(block[0], block[1], block[2], cols, length, first, first_col, sem),
            fetch(outer[0], outer[1], outer[2], reach, length, first, outer_col, sem + 1),
            fetch(inner[0], inner[1], inner[2], reach, length, first, inner_col, sem + 2),
        ]

    plain, other, chosen = [], [], []
    special = None
    if stage == EARLY:
        plain = part(0, rows, (own, 0, 0), (outer_both, 0, 0), (inner_both, 0, 0), 0)
    elif stage == MIDDLE:
        other = part(rows, rows, (near, 0, 0), (outer_near, 0, 0), (inner_near, 0, 0), 0)
        chosen = part(rows, rows, (melt, 0, 0), (outer_both, rows, 0), (inner_both, rows, 0), 0)
        special = at_end
    else:
        half = reach // 2
        other = [fetch(inner_far, 0, 0, reach, reach, 2 * rows, inner_col, 2)]
        for i, far in enumerate((far_low, far_high)):
            first = 2 * rows + i * half
            other.append(fetch(far, 0, 0, cols, half, first, first_col, 5 + i))
            other.append(fetch(far, 0, cols, reach, half, first, outer_col, i))
        chosen = part(2 * rows, reach, (melt, 0, 0), (outer_both, rows, 0), (inner_both, rows, 0), 0)
        special = next_end

    def each(act):
        for copy in plain:
            act(copy)
        if special is None:
            return

        @pl.when(special)
        def _():
            for copy in chosen:
                act(copy)

        @pl.when(jnp.logical_not(special))
        def _():
            for copy in other:
                act(copy)

    each(lambda copy: copy.start())
    if stage != LATE:
        token[...] = jnp.zeros_like(token)
    if stage == EARLY:
        for field in range(3):
            for buffer in (even, odd):
                buffer[field, zero_slot] = jnp.zeros_like(buffer[field, zero_slot])
    if stage == LATE:
        half = rows // 2
        first_half = pltpu.make_async_copy(
            even.at[:, pl.ds(2 * reach, half), pl.ds(first_col, cols)], out.at[:, pl.ds(0, half)], sems.at[7]
        )
        first_half.start()
    each(lambda copy: copy.wait())

    first_missing = reach - extra + rows
    second_missing = reach - extra + 2 * rows

    def substep(k, source, target, cursor):
        next_cursor = cursor + slide_ref[k]
        top = cursor + total_rows - base
        bottom = next_cursor - base
        if stage == EARLY:
            low, high = reach + k + 1, first_missing - 1 - k
        elif stage == MIDDLE:
            low, high = jnp.maximum(first_missing - 1 - k, reach + k + 1), second_missing - 1 - k
        else:
            low, high = second_missing - 1 - k, reach + count - 1 - k

        def advance(j, carry):
            r = low + group * j if stage == LATE else high - group * (j + 1)
            slots = [r - 1, r] + [jnp.where(r + q < top, r + q, zero_slot) for q in range(1, group + 1)]
            for t in range(tiles):
                s0 = first_row + TILE * t
                centre = [[source[f, slot, pl.ds(s0, TILE)] for slot in slots] for f in range(3)]
                for i in range(group):
                    slot = slots[1 + i]
                    value, around = [], []
                    for f in range(3):
                        c = centre[f][1 + i]
                        around.append(
                            (centre[f][i] + centre[f][i + 2])
                            + (source[f, slot, pl.ds(s0 - 1, TILE)] + source[f, slot, pl.ds(s0 + 1, TILE)])
                            + (pltpu.roll(c, 1, 1) + pltpu.roll(c, c.shape[1] - 1, 1))
                        )
                        value.append(c)
                    phase, solute, heat = value
                    squared = phase * phase
                    rest = 1.0 - squared
                    drive = (
                        coef_phase * around[0]
                        + phase * ((1.0 - 6.0 * coef_phase + coef_react) - coef_react * squared)
                        - (rest * rest) * (coef_couple * heat + (coef_couple * coef_solute) * solute)
                    )
                    grown = jnp.tanh(drive)
                    change = 0.5 * (grown - phase)
                    result = [
                        grown,
                        (1.0 - 6.0 * coef_diff) * solute + (coef_diff * around[1] + change),
                        (1.0 - 6.0 * coef_heat) * heat + (coef_heat * around[2] + change),
                    ]
                    if t == 0:
                        result = [jnp.where(low_inside, v, 0.0) for v in result]
                    if t == tiles - 1:
                        result = [jnp.where(high_inside, v, 0.0) for v in result]
                    for f in range(3):
                        target[f, r + i, pl.ds(s0, TILE)] = result[f]
            return carry

        lax.fori_loop(0, jnp.maximum(high - low + group - 1, 0) // group, advance, 0)

        span = pl.ds(first_row, TILE * tiles)

        def clear(r, carry):
            for f in range(3):
                target[f, r, span] = jnp.zeros_like(target[f, r, span])
            return carry

        def keep(r, carry):
            for f in range(3):
                target[f, r, span] = source[f, r, span]
            return carry

        lax.fori_loop(low, jnp.clip(bottom, low, jnp.maximum(high, low)), clear, 0)
        lax.fori_loop(jnp.clip(top, low, jnp.maximum(high, low)), high, keep, 0)
        return next_cursor

    def pair(j, cursor):
        return substep(2 * j + 1, odd, even, substep(2 * j, even, odd, cursor))

    lax.fori_loop(0, steps // 2, pair, jnp.int32(0))

    if stage == LATE:
        second_half = pltpu.make_async_copy(
            even.at[:, pl.ds(2 * reach + half, rows - half), pl.ds(first_col, cols)],
            out.at[:, pl.ds(half, rows - half)],
            sems.at[4],
        )
        second_half.start()
        first_half.wait()
        second_half.wait()


def pack_kernel(plan, *refs):
    sources, targets, sems = refs[: plan[0]], refs[plan[0] : -1], refs[-1]
    wide_index = lax.axis_index("wide")
    copies = []
    for i, (source, target, planes, cols, into, side) in enumerate(plan[1]):
        start, width = cols
        if side is not None:
            first, last = (start, width) if side == "inner" else (width, start)
            start = pl.multiple_of(jnp.where(lax.rem(wide_index, 2) == 0, last, first), TILE)
            width = into[3]
        copies.append(
            pltpu.make_async_copy(
                sources[source].at[:, pl.ds(*planes), pl.ds(start, width)],
                targets[target].at[:, pl.ds(into[0], into[1]), pl.ds(into[2], into[3])],
                sems.at[i],
            )
        )
    for copy in copies:
        copy.start()
    for copy in copies:
        copy.wait()


def place(arrays):
    sources, specs = [], []
    for array, space in arrays:
        sources.append(pltpu.with_memory_space_constraint(array, space))
        specs.append(pl.BlockSpec(memory_space=space))
    return sources, specs


def pack(name, sources, shapes, moves, cost=1000):
    sources, specs = place(sources)
    return pl.pallas_call(
        functools.partial(pack_kernel, (len(sources), moves)),
        out_shape=[pltpu.VMEM(shape, jnp.float32) for shape in shapes],
        in_specs=specs,
        out_specs=[pl.BlockSpec(memory_space=pltpu.VMEM)] * len(shapes),
        scratch_shapes=[pltpu.SemaphoreType.DMA((len(moves),))],
        cost_estimate=pl.CostEstimate(flops=0, bytes_accessed=cost, transcendentals=0),
        compiler_params=pltpu.CompilerParams(vmem_limit_bytes=4 * 1024 * 1024),
        name=name,
    )(*sources)


def run_stage(stage, shape, slide_planes, arrays, state=()):
    _, rows, cols, depth = shape
    reach = slide_planes.shape[0]
    anywhere = pl.BlockSpec(memory_space=pl.ANY)
    in_vmem = pl.BlockSpec(memory_space=pltpu.VMEM)
    held = pltpu.VMEM((3, rows + 4 * reach + 1, cols + 4 * TILE, depth), jnp.float32)
    operands, in_specs = place(arrays + [(s, pltpu.VMEM) for s in state])
    operands, in_specs = [slide_planes] + operands, [pl.BlockSpec(memory_space=pltpu.SMEM)] + in_specs
    out_shape, out_specs = [held, held], [in_vmem, in_vmem]
    if stage != LATE:
        out_shape, out_specs = [held, held, pltpu.VMEM((TILE, depth), jnp.float32)], [in_vmem] * 3
    if stage == LATE:
        out_shape, out_specs = [jax.ShapeDtypeStruct(shape, jnp.float32)] + out_shape, [anywhere] + out_specs
    offset = 1 if stage == LATE else 0
    aliases = {len(operands) - 2 + i: offset + i for i in range(2)} if state else {}
    return pl.pallas_call(
        functools.partial(stage_kernel, stage, rows, cols),
        out_shape=out_shape,
        in_specs=in_specs,
        out_specs=out_specs,
        input_output_aliases=aliases,
        scratch_shapes=[pltpu.SemaphoreType.DMA((8,))],
        cost_estimate=pl.CostEstimate(flops=0, bytes_accessed=1000, transcendentals=0),
        compiler_params=pltpu.CompilerParams(vmem_limit_bytes=16 * 1024 * 1024),
        name=("early", "middle", "late")[stage],
    )(*operands)


def body(fields, melt_planes, slide_planes):
    rows, cols, depth = fields.shape[1:]
    reach = slide_planes.shape[0]
    split = rows // 2
    wide = lax.axis_size("wide")
    inner_pairs = [(a, a + 1) for a in range(0, wide - 1, 2)]
    outer_pairs = [(a, a + 1) for a in range(1, wide - 1, 2)]
    is_even = lax.rem(lax.axis_index("wide"), 2) == 0
    inner_start = jnp.where(is_even, cols - reach, 0)

    def edge(block):
        return lax.dynamic_slice_in_dim(block, inner_start, reach, 2)

    def far_away(array):
        return (array, pltpu.HBM)

    def close(array):
        return (array, pltpu.VMEM)

    ends = (0, cols - reach)
    half = reach // 2
    spare = half * (cols + reach) // reach + 1 - rows
    near = passed(fields, -1)
    outer_own, outer_pair, inner_pair = pack(
        "pack_strips",
        [far_away(fields), far_away(melt_planes)],
        [(3, rows + spare, reach, depth), (3, 2 * rows, reach, depth), (3, 2 * rows, reach, depth)],
        [
            (0, 0, (0, rows), ends, (0, rows, 0, reach), "outer"),
            (0, 0, (0, spare), ends, (rows, spare, 0, reach), "outer"),
            (0, 1, (0, rows), ends, (0, rows, 0, reach), "outer"),
            (1, 1, (0, rows), ends, (rows, rows, 0, reach), "outer"),
            (0, 2, (0, rows), ends, (0, rows, 0, reach), "inner"),
            (1, 2, (0, rows), ends, (rows, rows, 0, reach), "inner"),
        ],
    )
    outer_near = passed(outer_own, -1, outer_pairs)
    outer_both = passed(outer_pair, 0, outer_pairs)
    inner_both = passed(inner_pair, 0, inner_pairs)
    far_low, far_high = pack(
        "pack_far",
        [far_away(fields), close(outer_both)],
        [(3, half, cols + reach, depth)] * 2,
        [
            (0, 0, (0, half), (0, cols), (0, half, 0, cols), None),
            (1, 0, (0, half), (0, reach), (0, half, cols, reach), None),
            (0, 1, (half, half), (0, cols), (0, half, 0, cols), None),
            (1, 1, (half, half), (0, reach), (0, half, cols, reach), None),
        ],
    )
    far_low, far_high = passed(far_low, -2), passed(far_high, -2)
    run = functools.partial(run_stage, shape=fields.shape, slide_planes=slide_planes)
    both = [close(outer_both), close(inner_both)]
    *state, token = run(EARLY, arrays=[far_away(fields), *both])
    (near_edge,) = pack(
        "pack_edge",
        [close(near), close(token)],
        [(3, rows, reach, depth)],
        [(0, 0, (0, rows), ends, (0, rows, 0, reach), "inner")],
    )
    inner_near = passed(near_edge, 0, inner_pairs)
    *state, token = run(
        MIDDLE, arrays=[close(near), far_away(melt_planes), *both, close(outer_near), close(inner_near)], state=state
    )
    (far_inner,) = pack(
        "pack_edge",
        [close(far_low), close(far_high), close(token)],
        [(3, reach, reach, depth)],
        [
            (0, 0, (0, half), ends, (0, half, 0, reach), "inner"),
            (1, 0, (0, half), ends, (half, half, 0, reach), "inner"),
        ],
    )
    inner_far = passed(far_inner, 0, inner_pairs)
    return run(LATE, arrays=[close(far_low), close(far_high), close(inner_far), far_away(melt_planes), *both], state=state)[0]


def solution(mesh):
    return jax.shard_map(
        body,
        mesh=mesh,
        in_specs=(P(None, "grow", "wide", None), P(None, None, "wide", None), P()),
        out_specs=P(None, "grow", "wide", None),
        check_vma=False,
    )
```

```python
import functools

import jax
import jax.numpy as jnp
from jax import lax
from jax.experimental import pallas as pl
from jax.experimental.pallas import tpu as pltpu
from jax.sharding import PartitionSpec as P

TILE = 8
EARLY, MIDDLE, LATE = 0, 1, 2
GROUPS = ((6,), (16,), (8, 4))
PIECES = 2
MIDDLE_FLOPS = 3_500_000_000

coef_phase = 0.15
coef_react = 0.3
coef_couple = 0.4
coef_solute = 1.5
coef_diff = 0.1
coef_heat = 0.16


def passed(value, grow_step, wide_pairs=None):
    grow, wide = lax.axis_size("grow"), lax.axis_size("wide")
    if wide_pairs is None:
        return lax.ppermute(value, "grow", [(g, g + grow_step) for g in range(grow) if 0 <= g + grow_step < grow])
    lanes = wide_pairs + [(b, a) for a, b in wide_pairs]
    if grow_step == 0:
        return lax.ppermute(value, "wide", lanes)
    pairs = [
        (g * wide + a, (g + grow_step) * wide + b)
        for g in range(grow)
        if 0 <= g + grow_step < grow
        for a, b in lanes
    ]
    return lax.ppermute(value, ("grow", "wide"), pairs)


def stage_kernel(stage, rows, cols, slide_ref, *refs):
    steps = slide_ref.shape[0]
    reach = steps
    count = rows + 2 * reach
    zero_slot = count + 2 * reach
    first_col = 2 * TILE
    first_row = first_col - reach
    tiles = cols // TILE + 2 * (reach // TILE)
    total_rows = rows * lax.axis_size("grow")
    grow_index, wide_index = lax.axis_index("grow"), lax.axis_index("wide")
    at_end = grow_index == lax.axis_size("grow") - 1
    next_end = grow_index == lax.axis_size("grow") - 2
    is_even = lax.rem(wide_index, 2) == 0
    low_inside = wide_index > 0
    high_inside = wide_index < lax.axis_size("wide") - 1

    total = slide_ref[0]
    for k in range(1, steps):
        total = total + slide_ref[k]
    extra = total - reach
    base = grow_index * rows + extra - reach
    low_col, high_col = first_row, first_col + cols
    outer_col = pl.multiple_of(jnp.where(is_even, low_col, high_col), TILE)
    inner_col = pl.multiple_of(jnp.where(is_even, high_col, low_col), TILE)

    if stage == EARLY:
        own, outer_both, inner_both, even, odd, token, sems = refs
    elif stage == MIDDLE:
        near, melt, outer_both, inner_both, outer_near, *inner_near, _, _, even, odd, token, sems = refs
    else:
        far, melt, outer_both, inner_both, _, _, out, even, odd, sems = refs

    def fetch(source, start, col_from, width, length, first, col, sem):
        return pltpu.make_async_copy(
            source.at[:, pl.ds(start, length), pl.ds(col_from, width)],
            even.at[:, pl.ds(reach - extra + first, length), pl.ds(col, width)],
            sems.at[sem],
        )

    def part(first, length, block, outer, inner, sem):
        return [
            fetch(block[0], block[1], block[2], cols, length, first, first_col, sem),
            fetch(outer[0], outer[1], outer[2], reach, length, first, outer_col, sem + 1),
            fetch(inner[0], inner[1], inner[2], reach, length, first, inner_col, sem + 2),
        ]

    plain, other, chosen = [], [], []
    special = None
    if stage == EARLY:
        plain = part(0, rows, (own, 0, 0), (outer_both, 0, 0), (inner_both, 0, 0), 0)
    elif stage == MIDDLE:
        size = rows // PIECES
        other = [
            fetch(near, 0, 0, cols, rows, rows, first_col, 0),
            fetch(outer_near, 0, 0, reach, rows, rows, outer_col, 1),
        ] + [fetch(piece, 0, 0, reach, size, rows + i * size, inner_col, 8 + i) for i, piece in enumerate(inner_near)]
        chosen = part(rows, rows, (melt, 0, 0), (outer_both, rows, 0), (inner_both, rows, 0), 0)
        special = at_end
    else:
        other = [fetch(far, 0, 0, cols, reach, 2 * rows, first_col, 0)]
        chosen = part(2 * rows, reach, (melt, 0, 0), (outer_both, rows, 0), (inner_both, rows, 0), 0)
        special = next_end

    def each(act):
        for copy in plain:
            act(copy)
        if special is None:
            return

        @pl.when(special)
        def _():
            for copy in chosen:
                act(copy)

        @pl.when(jnp.logical_not(special))
        def _():
            for copy in other:
                act(copy)

    each(lambda copy: copy.start())
    if stage != LATE:
        token[...] = jnp.zeros_like(token)
    if stage == EARLY:
        for field in range(3):
            for buffer in (even, odd):
                buffer[field, zero_slot] = jnp.zeros_like(buffer[field, zero_slot])
    if stage == LATE:
        half = rows // 2
        first_half = pltpu.make_async_copy(
            even.at[:, pl.ds(2 * reach, half), pl.ds(first_col, cols)], out.at[:, pl.ds(0, half)], sems.at[3]
        )
        first_half.start()
        single = [
            pltpu.make_async_copy(
                even.at[:, pl.ds(2 * reach + p, 1), pl.ds(first_col, cols)], out.at[:, pl.ds(p, 1)], sems.at[8 + p - half]
            )
            for p in range(half, rows)
        ]
        for p, copy in enumerate(single):
            pl.when(p < rows - half - extra)(copy.start)

        @pl.when(jnp.logical_not(next_end))
        def _():
            slot = reach - extra + 2 * rows
            for side, (col, low_side) in enumerate(((outer_col, is_even), (inner_col, jnp.logical_not(is_even)))):
                for q in range(reach // 2):
                    for f in range(3):
                        packed = far[f, reach + side, pl.ds(q * reach, reach)]
                        even[f, slot + q, pl.ds(col, reach)] = packed
                        even[f, slot + reach - 1 - q, pl.ds(col, reach)] = turned(packed, q, jnp.logical_not(low_side))
    each(lambda copy: copy.wait())

    first_missing = reach - extra + rows
    second_missing = reach - extra + 2 * rows

    def substep(k, source, target, cursor, trim):
        rows_in = (tiles * TILE - 2 * trim) // TILE
        next_cursor = cursor + slide_ref[k]
        top = cursor + total_rows - base
        bottom = next_cursor - base
        if stage == EARLY:
            low, high = reach + k + 1, first_missing - 1 - k
        elif stage == MIDDLE:
            low, high = jnp.maximum(first_missing - 1 - k, reach + k + 1), second_missing - 1 - k
        else:
            low, high = second_missing - 1 - k, reach + count - 1 - k

        def advance(group, first, j, carry):
            r = first + group * j if stage == LATE else high - group * (j + 1)
            slots = [r - 1, r] + [jnp.where(r + q < top, r + q, zero_slot) for q in range(1, group + 1)]
            for t in range(rows_in):
                s0 = first_row + trim + TILE * t
                centre = [[source[f, slot, pl.ds(s0, TILE)] for slot in slots] for f in range(3)]
                for i in range(group):
                    slot = slots[1 + i]
                    value, around = [], []
                    for f in range(3):
                        c = centre[f][1 + i]
                        around.append(
                            (centre[f][i] + centre[f][i + 2])
                            + (source[f, slot, pl.ds(s0 - 1, TILE)] + source[f, slot, pl.ds(s0 + 1, TILE)])
                            + (pltpu.roll(c, 1, 1) + pltpu.roll(c, c.shape[1] - 1, 1))
                        )
                        value.append(c)
                    phase, solute, heat = value
                    squared = phase * phase
                    rest = 1.0 - squared
                    drive = (
                        coef_phase * around[0]
                        + phase * ((1.0 - 6.0 * coef_phase + coef_react) - coef_react * squared)
                        - (rest * rest) * (coef_couple * heat + (coef_couple * coef_solute) * solute)
                    )
                    grown = jnp.tanh(drive)
                    change = 0.5 * (grown - phase)
                    result = [
                        grown,
                        (1.0 - 6.0 * coef_diff) * solute + (coef_diff * around[1] + change),
                        (1.0 - 6.0 * coef_heat) * heat + (coef_heat * around[2] + change),
                    ]
                    if t == 0:
                        result = [jnp.where(keep_low[trim], v, 0.0) for v in result]
                    if t == rows_in - 1:
                        result = [jnp.where(keep_high[trim], v, 0.0) for v in result]
                    for f in range(3):
                        target[f, r + i, pl.ds(s0, TILE)] = result[f]
            return carry

        first = low
        for group in GROUPS[stage]:
            smallest = GROUPS[stage][-1]
            times = jnp.maximum(high - first + smallest - 1, 0) // group
            lax.fori_loop(0, times, functools.partial(advance, group, first), 0)
            first = first + group * times

        span = pl.ds(first_row, TILE * tiles)

        def clear(r, carry):
            for f in range(3):
                target[f, r, span] = jnp.zeros_like(target[f, r, span])
            return carry

        def keep(r, carry):
            for f in range(3):
                target[f, r, span] = source[f, r, span]
            return carry

        lax.fori_loop(low, jnp.clip(bottom, low, jnp.maximum(high, low)), clear, 0)
        lax.fori_loop(jnp.clip(top, low, jnp.maximum(high, low)), high, keep, 0)
        return next_cursor

    row = lax.broadcasted_iota(jnp.int32, (TILE, even.shape[3]), 0)
    half_tile = TILE // 2
    keep_low = {0: low_inside, half_tile: low_inside | (row >= half_tile)}
    keep_high = {0: high_inside, half_tile: high_inside | (row < half_tile)}

    def pair(trim):
        def run(j, cursor):
            return substep(2 * j + 1, odd, even, substep(2 * j, even, odd, cursor, trim), trim)

        return run

    wide_pairs = (steps - half_tile) // 2
    cursor = lax.fori_loop(0, wide_pairs, pair(0), jnp.int32(0))
    lax.fori_loop(wide_pairs, steps // 2, pair(half_tile), cursor)

    if stage == LATE:
        for p, copy in enumerate(single):
            pl.when(p >= rows - half - extra)(copy.start)
        first_half.wait()
        for copy in single:
            copy.wait()


def pack_kernel(plan, *refs):
    sources, targets, sems = refs[: plan[0]], refs[plan[0] : -1], refs[-1]
    wide_index = lax.axis_index("wide")
    copies = []
    for i, (source, target, planes, cols, into, side) in enumerate(plan[1]):
        start, width = cols
        if side is not None:
            first, last = (start, width) if side == "inner" else (width, start)
            start = pl.multiple_of(jnp.where(lax.rem(wide_index, 2) == 0, last, first), TILE)
            width = into[3]
        copies.append(
            pltpu.make_async_copy(
                sources[source].at[:, pl.ds(*planes), pl.ds(start, width)],
                targets[target].at[:, pl.ds(into[0], into[1]), pl.ds(into[2], into[3])],
                sems.at[i],
            )
        )
    for copy in copies:
        copy.start()
    for copy in copies:
        copy.wait()


def turned(rows, count, down):
    if count == 0:
        return rows
    return jnp.where(down, pltpu.roll(rows, count, 0), pltpu.roll(rows, rows.shape[0] - count, 0))


def pack_far_kernel(fields, outer, inner, _, block, sem):
    reach, cols = outer.shape[2], fields.shape[2]
    copy = pltpu.make_async_copy(fields.at[:, pl.ds(0, reach)], block.at[:, pl.ds(0, reach)], sem)
    copy.start()
    is_even = lax.rem(lax.axis_index("wide"), 2) == 0
    row = lax.broadcasted_iota(jnp.int32, (reach, fields.shape[3]), 0)
    for side, (strip, low_side) in enumerate(((outer, is_even), (inner, jnp.logical_not(is_even)))):
        for q in range(cols // reach):
            if q >= reach // 2:
                block[:, reach + side, pl.ds(q * reach, reach)] = jnp.zeros((3, reach, fields.shape[3]), jnp.float32)
                continue
            near_rows = (low_side & (row > q)) | (jnp.logical_not(low_side) & (row < reach - 1 - q))
            for f in range(3):
                second = turned(strip[f, reach - 1 - q], q, low_side)
                block[f, reach + side, pl.ds(q * reach, reach)] = jnp.where(near_rows, strip[f, q], second)
    copy.wait()


def pack_far(fields, outer, inner, token):
    reach, (_, _, cols, depth) = outer.shape[2], fields.shape
    operands, specs = place([(fields, pltpu.HBM), (outer, pltpu.VMEM), (inner, pltpu.VMEM), (token, pltpu.VMEM)])
    return pl.pallas_call(
        pack_far_kernel,
        out_shape=pltpu.VMEM((3, reach + 2, cols, depth), jnp.float32),
        in_specs=specs,
        out_specs=pl.BlockSpec(memory_space=pltpu.VMEM),
        scratch_shapes=[pltpu.SemaphoreType.DMA],
        cost_estimate=pl.CostEstimate(flops=0, bytes_accessed=1000, transcendentals=0),
        compiler_params=pltpu.CompilerParams(vmem_limit_bytes=4 * 1024 * 1024),
        name="pack_far",
    )(*operands)


def place(arrays):
    sources, specs = [], []
    for array, space in arrays:
        sources.append(pltpu.with_memory_space_constraint(array, space))
        specs.append(pl.BlockSpec(memory_space=space))
    return sources, specs


def pack(name, sources, shapes, moves, cost=1000):
    sources, specs = place(sources)
    return pl.pallas_call(
        functools.partial(pack_kernel, (len(sources), moves)),
        out_shape=[pltpu.VMEM(shape, jnp.float32) for shape in shapes],
        in_specs=specs,
        out_specs=[pl.BlockSpec(memory_space=pltpu.VMEM)] * len(shapes),
        scratch_shapes=[pltpu.SemaphoreType.DMA((len(moves),))],
        cost_estimate=pl.CostEstimate(flops=0, bytes_accessed=cost, transcendentals=0),
        compiler_params=pltpu.CompilerParams(vmem_limit_bytes=4 * 1024 * 1024),
        name=name,
    )(*sources)


def run_stage(stage, shape, slide_planes, arrays, state=()):
    _, rows, cols, depth = shape
    reach = slide_planes.shape[0]
    anywhere = pl.BlockSpec(memory_space=pl.ANY)
    in_vmem = pl.BlockSpec(memory_space=pltpu.VMEM)
    held = pltpu.VMEM((3, rows + 4 * reach + 1, cols + 4 * TILE, depth), jnp.float32)
    operands, in_specs = place(arrays + [(s, pltpu.VMEM) for s in state])
    operands, in_specs = [slide_planes] + operands, [pl.BlockSpec(memory_space=pltpu.SMEM)] + in_specs
    out_shape, out_specs = [held, held], [in_vmem, in_vmem]
    if stage != LATE:
        out_shape, out_specs = [held, held, pltpu.VMEM((TILE, depth), jnp.float32)], [in_vmem] * 3
    if stage == LATE:
        out_shape, out_specs = [jax.ShapeDtypeStruct(shape, jnp.float32)] + out_shape, [anywhere] + out_specs
    offset = 1 if stage == LATE else 0
    aliases = {len(operands) - 2 + i: offset + i for i in range(2)} if state else {}
    return pl.pallas_call(
        functools.partial(stage_kernel, stage, rows, cols),
        out_shape=out_shape,
        in_specs=in_specs,
        out_specs=out_specs,
        input_output_aliases=aliases,
        scratch_shapes=[pltpu.SemaphoreType.DMA((8 + max(PIECES, rows // 2),))],
        cost_estimate=pl.CostEstimate(flops=MIDDLE_FLOPS if stage == MIDDLE else 0, bytes_accessed=1000, transcendentals=0),
        compiler_params=pltpu.CompilerParams(vmem_limit_bytes=16 * 1024 * 1024),
        name=("early", "middle", "late")[stage],
    )(*operands)


def body(fields, melt_planes, slide_planes):
    rows, cols, depth = fields.shape[1:]
    reach = slide_planes.shape[0]
    split = rows // 2
    wide = lax.axis_size("wide")
    inner_pairs = [(a, a + 1) for a in range(0, wide - 1, 2)]
    outer_pairs = [(a, a + 1) for a in range(1, wide - 1, 2)]
    is_even = lax.rem(lax.axis_index("wide"), 2) == 0
    inner_start = jnp.where(is_even, cols - reach, 0)

    def edge(block):
        return lax.dynamic_slice_in_dim(block, inner_start, reach, 2)

    def far_away(array):
        return (array, pltpu.HBM)

    def close(array):
        return (array, pltpu.VMEM)

    ends = (0, cols - reach)
    near = passed(fields, -1)
    outer_own, outer_pair, inner_pair = pack(
        "pack_strips",
        [far_away(fields), far_away(melt_planes)],
        [(3, rows, reach, depth), (3, 2 * rows, reach, depth), (3, 2 * rows, reach, depth)],
        [
            (0, 0, (0, rows), ends, (0, rows, 0, reach), "outer"),
            (0, 1, (0, rows), ends, (0, rows, 0, reach), "outer"),
            (1, 1, (0, rows), ends, (rows, rows, 0, reach), "outer"),
            (0, 2, (0, rows), ends, (0, rows, 0, reach), "inner"),
            (1, 2, (0, rows), ends, (rows, rows, 0, reach), "inner"),
        ],
    )
    outer_near = passed(outer_own, -1, outer_pairs)
    outer_both = passed(outer_pair, 0, outer_pairs)
    inner_both = passed(inner_pair, 0, inner_pairs)
    run = functools.partial(run_stage, shape=fields.shape, slide_planes=slide_planes)
    both = [close(outer_both), close(inner_both)]
    *state, token = run(EARLY, arrays=[far_away(fields), *both])
    far_block = pack_far(fields, outer_both, inner_both, token)
    far = passed(far_block, -2)
    size = rows // PIECES
    edges = pack(
        "pack_edge",
        [close(near), close(token)],
        [(3, size, reach, depth)] * PIECES,
        [(0, i, (i * size, size), ends, (0, size, 0, reach), "inner") for i in range(PIECES)],
    )
    inner_near = [close(passed(piece, 0, inner_pairs)) for piece in edges]
    *state, _ = run(
        MIDDLE, arrays=[close(near), far_away(melt_planes), *both, close(outer_near), *inner_near], state=state
    )
    return run(LATE, arrays=[close(far), far_away(melt_planes), *both], state=state)[0]


def solution(mesh):
    return jax.shard_map(
        body,
        mesh=mesh,
        in_specs=(P(None, "grow", "wide", None), P(None, None, "wide", None), P()),
        out_specs=P(None, "grow", "wide", None),
        check_vma=False,
    )
```

```python
import functools

import jax
import jax.numpy as jnp
from jax import lax
from jax.experimental import pallas as pl
from jax.experimental.pallas import tpu as pltpu
from jax.sharding import PartitionSpec as P

TILE = 8
EARLY, MIDDLE, LATE = 0, 1, 2
GROUPS = ((6,), (16,), (8, 4, 2))
PIECES = 2
MIDDLE_FLOPS = 3_500_000_000

coef_phase = 0.15
coef_react = 0.3
coef_couple = 0.4
coef_solute = 1.5
coef_diff = 0.1
coef_heat = 0.16


def passed(value, grow_step, wide_pairs=None):
    grow, wide = lax.axis_size("grow"), lax.axis_size("wide")
    if wide_pairs is None:
        return lax.ppermute(value, "grow", [(g, g + grow_step) for g in range(grow) if 0 <= g + grow_step < grow])
    lanes = wide_pairs + [(b, a) for a, b in wide_pairs]
    if grow_step == 0:
        return lax.ppermute(value, "wide", lanes)
    pairs = [
        (g * wide + a, (g + grow_step) * wide + b)
        for g in range(grow)
        if 0 <= g + grow_step < grow
        for a, b in lanes
    ]
    return lax.ppermute(value, ("grow", "wide"), pairs)


def stage_kernel(stage, rows, cols, slide_rows, *refs):
    *refs, slide_ref = refs
    steps = slide_ref.shape[0]
    reach = steps
    count = rows + 2 * reach
    zero_slot = count + 2 * reach
    first_col = 2 * TILE
    first_row = first_col - reach
    tiles = cols // TILE + 2 * (reach // TILE)
    total_rows = rows * lax.axis_size("grow")
    grow_index, wide_index = lax.axis_index("grow"), lax.axis_index("wide")
    at_end = grow_index == lax.axis_size("grow") - 1
    next_end = grow_index == lax.axis_size("grow") - 2
    is_even = lax.rem(wide_index, 2) == 0
    low_inside = wide_index > 0
    high_inside = wide_index < lax.axis_size("wide") - 1

    slides = slide_rows[...]
    total = jnp.int32(0)
    for k in range(steps):
        shift = slides[k, 0]
        slide_ref[k] = shift
        total = total + shift
    extra = total - reach
    base = grow_index * rows + extra - reach
    low_col, high_col = first_row, first_col + cols
    outer_col = pl.multiple_of(jnp.where(is_even, low_col, high_col), TILE)
    inner_col = pl.multiple_of(jnp.where(is_even, high_col, low_col), TILE)

    if stage == EARLY:
        own, outer_both, inner_both, even, odd, token, sems = refs
    elif stage == MIDDLE:
        near, melt, outer_both, inner_both, outer_near, *inner_near, _, _, even, odd, token, sems = refs
    else:
        far, melt, outer_both, inner_both, _, _, out, even, odd, sems = refs

    def fetch(source, start, col_from, width, length, first, col, sem):
        return pltpu.make_async_copy(
            source.at[:, pl.ds(start, length), pl.ds(col_from, width)],
            even.at[:, pl.ds(reach - extra + first, length), pl.ds(col, width)],
            sems.at[sem],
        )

    def part(first, length, block, outer, inner, sem):
        return [
            fetch(block[0], block[1], block[2], cols, length, first, first_col, sem),
            fetch(outer[0], outer[1], outer[2], reach, length, first, outer_col, sem + 1),
            fetch(inner[0], inner[1], inner[2], reach, length, first, inner_col, sem + 2),
        ]

    def move(source, start, col_from, width, length, first, col):
        def one(i, carry):
            for f in range(3):
                even[f, reach - extra + first + i, pl.ds(col, width)] = source[f, start + i, pl.ds(col_from, width)]
            return carry

        lax.fori_loop(0, length, one, 0, unroll=4)

    def moves():
        if stage == MIDDLE:
            size = rows // PIECES
            move(near, 0, 0, cols, rows, rows, first_col)
            move(outer_near, 0, 0, reach, rows, rows, outer_col)
            for i, piece in enumerate(inner_near):
                move(piece, 0, 0, reach, size, rows + i * size, inner_col)
        elif stage == LATE:
            move(far, 0, 0, cols, reach, 2 * rows, first_col)
            slot = reach - extra + 2 * rows
            for side, (col, low_side) in enumerate(((outer_col, is_even), (inner_col, jnp.logical_not(is_even)))):
                for q in range(reach // 2):
                    for f in range(3):
                        packed = far[f, reach + side, pl.ds(q * reach, reach)]
                        even[f, slot + q, pl.ds(col, reach)] = packed
                        even[f, slot + reach - 1 - q, pl.ds(col, reach)] = turned(packed, q, jnp.logical_not(low_side))

    plain, chosen, special = [], [], None
    if stage == EARLY:
        plain = part(0, rows, (own, 0, 0), (outer_both, 0, 0), (inner_both, 0, 0), 0)
    elif stage == MIDDLE:
        chosen = part(rows, rows, (melt, 0, 0), (outer_both, rows, 0), (inner_both, rows, 0), 0)
        special = at_end
    else:
        chosen = part(2 * rows, reach, (melt, 0, 0), (outer_both, rows, 0), (inner_both, rows, 0), 0)
        special = next_end

    def each(act):
        for copy in plain:
            act(copy)
        if special is None:
            return

        @pl.when(special)
        def _():
            for copy in chosen:
                act(copy)

    each(lambda copy: copy.start())
    if stage != LATE:
        token[...] = jnp.zeros_like(token)
    if stage == EARLY:
        for field in range(3):
            for buffer in (even, odd):
                buffer[field, zero_slot] = jnp.zeros_like(buffer[field, zero_slot])
    if stage == LATE:
        half = rows // 2
        first_half = pltpu.make_async_copy(
            even.at[:, pl.ds(2 * reach, half), pl.ds(first_col, cols)], out.at[:, pl.ds(0, half)], sems.at[3]
        )
        first_half.start()
        single = [
            pltpu.make_async_copy(
                even.at[:, pl.ds(2 * reach + p, 1), pl.ds(first_col, cols)], out.at[:, pl.ds(p, 1)], sems.at[8 + p - half]
            )
            for p in range(half, rows)
        ]
        for p, copy in enumerate(single):
            pl.when(p < rows - half - extra)(copy.start)

    if special is not None:
        pl.when(jnp.logical_not(special))(moves)
    each(lambda copy: copy.wait())

    first_missing = reach - extra + rows
    second_missing = reach - extra + 2 * rows

    def substep(k, source, target, cursor, trim):
        next_cursor = cursor + slide_ref[k]
        top = cursor + total_rows - base
        bottom = next_cursor - base
        if stage == EARLY:
            low, high = reach + k + 1, first_missing - 1 - k
        elif stage == MIDDLE:
            low, high = jnp.maximum(first_missing - 1 - k, reach + k + 1), second_missing - 1 - k
        else:
            low, high = second_missing - 1 - k, reach + count - 1 - k

        def advance(group, first, j, carry):
            cut = half_tile if stage == LATE and group <= half_tile else trim
            rows_in = (tiles * TILE - 2 * cut) // TILE
            r = first + group * j if stage == LATE else high - group * (j + 1)
            slots = [r - 1, r] + [jnp.where(r + q < top, r + q, zero_slot) for q in range(1, group + 1)]
            for t in range(rows_in):
                s0 = first_row + cut + TILE * t
                centre = [[source[f, slot, pl.ds(s0, TILE)] for slot in slots] for f in range(3)]
                for i in range(group):
                    slot = slots[1 + i]
                    value, around = [], []
                    for f in range(3):
                        c = centre[f][1 + i]
                        around.append(
                            (centre[f][i] + centre[f][i + 2])
                            + (source[f, slot, pl.ds(s0 - 1, TILE)] + source[f, slot, pl.ds(s0 + 1, TILE)])
                            + (pltpu.roll(c, 1, 1) + pltpu.roll(c, c.shape[1] - 1, 1))
                        )
                        value.append(c)
                    phase, solute, heat = value
                    squared = phase * phase
                    rest = 1.0 - squared
                    drive = (
                        coef_phase * around[0]
                        + phase * ((1.0 - 6.0 * coef_phase + coef_react) - coef_react * squared)
                        - (rest * rest) * (coef_couple * heat + (coef_couple * coef_solute) * solute)
                    )
                    grown = jnp.tanh(drive)
                    change = 0.5 * (grown - phase)
                    result = [
                        grown,
                        (1.0 - 6.0 * coef_diff) * solute + (coef_diff * around[1] + change),
                        (1.0 - 6.0 * coef_heat) * heat + (coef_heat * around[2] + change),
                    ]
                    if t == 0:
                        result = [jnp.where(keep_low[cut], v, 0.0) for v in result]
                    if t == rows_in - 1:
                        result = [jnp.where(keep_high[cut], v, 0.0) for v in result]
                    for f in range(3):
                        target[f, r + i, pl.ds(s0, TILE)] = result[f]
            return carry

        first = low
        for group, following in zip(GROUPS[stage], GROUPS[stage][1:] + GROUPS[stage][-1:]):
            times = jnp.maximum(high - first + following - 1, 0) // group
            lax.fori_loop(0, times, functools.partial(advance, group, first), 0)
            first = first + group * times

        span = pl.ds(first_row, TILE * tiles)

        def clear(r, carry):
            for f in range(3):
                target[f, r, span] = jnp.zeros_like(target[f, r, span])
            return carry

        def keep(r, carry):
            for f in range(3):
                target[f, r, span] = source[f, r, span]
            return carry

        high = jnp.maximum(high, low)

        @pl.when((bottom > low) | (top < high))
        def _():
            lax.fori_loop(low, jnp.clip(bottom, low, high), clear, 0)
            lax.fori_loop(jnp.clip(top, low, high), high, keep, 0)

        return next_cursor

    row = lax.broadcasted_iota(jnp.int32, (TILE, even.shape[3]), 0)
    half_tile = TILE // 2
    keep_low = {0: low_inside, half_tile: low_inside | (row >= half_tile)}
    keep_high = {0: high_inside, half_tile: high_inside | (row < half_tile)}

    def pair(trim):
        def run(j, cursor):
            return substep(2 * j + 1, odd, even, substep(2 * j, even, odd, cursor, trim), trim)

        return run

    wide_pairs = (steps - half_tile) // 2
    cursor = lax.fori_loop(0, wide_pairs, pair(0), jnp.int32(0))
    lax.fori_loop(wide_pairs, steps // 2, pair(half_tile), cursor)

    if stage == LATE:
        for p, copy in enumerate(single):
            pl.when(p >= rows - half - extra)(copy.start)
        first_half.wait()
        for copy in single:
            copy.wait()


def pack_kernel(plan, *refs):
    sources, targets, sems = refs[: plan[0]], refs[plan[0] : -1], refs[-1]
    wide_index = lax.axis_index("wide")
    copies = []
    for i, (source, target, planes, cols, into, side) in enumerate(plan[1]):
        start, width = cols
        if side is not None:
            first, last = (start, width) if side == "inner" else (width, start)
            start = pl.multiple_of(jnp.where(lax.rem(wide_index, 2) == 0, last, first), TILE)
            width = into[3]
        copies.append(
            pltpu.make_async_copy(
                sources[source].at[:, pl.ds(*planes), pl.ds(start, width)],
                targets[target].at[:, pl.ds(into[0], into[1]), pl.ds(into[2], into[3])],
                sems.at[i],
            )
        )
    for copy in copies:
        copy.start()
    for copy in copies:
        copy.wait()


def turned(rows, count, down):
    if count == 0:
        return rows
    return jnp.where(down, pltpu.roll(rows, count, 0), pltpu.roll(rows, rows.shape[0] - count, 0))


def pack_far_kernel(fields, outer, inner, _, block, sem):
    reach, cols = outer.shape[2], fields.shape[2]
    copy = pltpu.make_async_copy(fields.at[:, pl.ds(0, reach)], block.at[:, pl.ds(0, reach)], sem)
    copy.start()
    is_even = lax.rem(lax.axis_index("wide"), 2) == 0
    row = lax.broadcasted_iota(jnp.int32, (reach, fields.shape[3]), 0)
    for side, (strip, low_side) in enumerate(((outer, is_even), (inner, jnp.logical_not(is_even)))):
        for q in range(cols // reach):
            if q >= reach // 2:
                block[:, reach + side, pl.ds(q * reach, reach)] = jnp.zeros((3, reach, fields.shape[3]), jnp.float32)
                continue
            near_rows = (low_side & (row > q)) | (jnp.logical_not(low_side) & (row < reach - 1 - q))
            for f in range(3):
                second = turned(strip[f, reach - 1 - q], q, low_side)
                block[f, reach + side, pl.ds(q * reach, reach)] = jnp.where(near_rows, strip[f, q], second)
    copy.wait()


def pack_far(fields, outer, inner, token):
    reach, (_, _, cols, depth) = outer.shape[2], fields.shape
    operands, specs = place([(fields, pltpu.HBM), (outer, pltpu.VMEM), (inner, pltpu.VMEM), (token, pltpu.VMEM)])
    return pl.pallas_call(
        pack_far_kernel,
        out_shape=pltpu.VMEM((3, reach + 2, cols, depth), jnp.float32),
        in_specs=specs,
        out_specs=pl.BlockSpec(memory_space=pltpu.VMEM),
        scratch_shapes=[pltpu.SemaphoreType.DMA],
        cost_estimate=pl.CostEstimate(flops=0, bytes_accessed=1000, transcendentals=0),
        compiler_params=pltpu.CompilerParams(vmem_limit_bytes=4 * 1024 * 1024),
        name="pack_far",
    )(*operands)


def place(arrays):
    sources, specs = [], []
    for array, space in arrays:
        sources.append(pltpu.with_memory_space_constraint(array, space))
        specs.append(pl.BlockSpec(memory_space=space))
    return sources, specs


def pack(name, sources, shapes, moves, cost=1000):
    sources, specs = place(sources)
    return pl.pallas_call(
        functools.partial(pack_kernel, (len(sources), moves)),
        out_shape=[pltpu.VMEM(shape, jnp.float32) for shape in shapes],
        in_specs=specs,
        out_specs=[pl.BlockSpec(memory_space=pltpu.VMEM)] * len(shapes),
        scratch_shapes=[pltpu.SemaphoreType.DMA((len(moves),))],
        cost_estimate=pl.CostEstimate(flops=0, bytes_accessed=cost, transcendentals=0),
        compiler_params=pltpu.CompilerParams(vmem_limit_bytes=4 * 1024 * 1024),
        name=name,
    )(*sources)


def run_stage(stage, shape, slide_rows, arrays, state=()):
    _, rows, cols, depth = shape
    reach = slide_rows.shape[0]
    anywhere = pl.BlockSpec(memory_space=pl.ANY)
    in_vmem = pl.BlockSpec(memory_space=pltpu.VMEM)
    held = pltpu.VMEM((3, rows + 4 * reach + 1, cols + 4 * TILE, depth), jnp.float32)
    operands, in_specs = place([(slide_rows, pltpu.VMEM)] + arrays + [(s, pltpu.VMEM) for s in state])
    out_shape, out_specs = [held, held], [in_vmem, in_vmem]
    if stage != LATE:
        out_shape, out_specs = [held, held, pltpu.VMEM((TILE, depth), jnp.float32)], [in_vmem] * 3
    if stage == LATE:
        out_shape, out_specs = [jax.ShapeDtypeStruct(shape, jnp.float32)] + out_shape, [anywhere] + out_specs
    offset = 1 if stage == LATE else 0
    aliases = {len(operands) - 2 + i: offset + i for i in range(2)} if state else {}
    return pl.pallas_call(
        functools.partial(stage_kernel, stage, rows, cols),
        out_shape=out_shape,
        in_specs=in_specs,
        out_specs=out_specs,
        input_output_aliases=aliases,
        scratch_shapes=[pltpu.SemaphoreType.DMA((8 + max(PIECES, rows // 2),)), pltpu.SMEM((reach,), jnp.int32)],
        cost_estimate=pl.CostEstimate(flops=MIDDLE_FLOPS if stage == MIDDLE else 0, bytes_accessed=1000, transcendentals=0),
        compiler_params=pltpu.CompilerParams(vmem_limit_bytes=16 * 1024 * 1024),
        name=("early", "middle", "late")[stage],
    )(*operands)


def body(fields, melt_planes, slide_planes):
    rows, cols, depth = fields.shape[1:]
    reach = slide_planes.shape[0]
    split = rows // 2
    wide = lax.axis_size("wide")
    inner_pairs = [(a, a + 1) for a in range(0, wide - 1, 2)]
    outer_pairs = [(a, a + 1) for a in range(1, wide - 1, 2)]
    is_even = lax.rem(lax.axis_index("wide"), 2) == 0
    inner_start = jnp.where(is_even, cols - reach, 0)

    def edge(block):
        return lax.dynamic_slice_in_dim(block, inner_start, reach, 2)

    def far_away(array):
        return (array, pltpu.HBM)

    def close(array):
        return (array, pltpu.VMEM)

    ends = (0, cols - reach)
    near = passed(fields, -1)
    outer_own, outer_pair, inner_pair = pack(
        "pack_strips",
        [far_away(fields), far_away(melt_planes)],
        [(3, rows, reach, depth), (3, 2 * rows, reach, depth), (3, 2 * rows, reach, depth)],
        [
            (0, 0, (0, rows), ends, (0, rows, 0, reach), "outer"),
            (0, 1, (0, rows), ends, (0, rows, 0, reach), "outer"),
            (1, 1, (0, rows), ends, (rows, rows, 0, reach), "outer"),
            (0, 2, (0, rows), ends, (0, rows, 0, reach), "inner"),
            (1, 2, (0, rows), ends, (rows, rows, 0, reach), "inner"),
        ],
    )
    outer_near = passed(outer_own, -1, outer_pairs)
    outer_both = passed(outer_pair, 0, outer_pairs)
    inner_both = passed(inner_pair, 0, inner_pairs)
    slide_rows = jnp.broadcast_to(slide_planes[:, None], (reach, depth))
    run = functools.partial(run_stage, shape=fields.shape, slide_rows=slide_rows)
    both = [close(outer_both), close(inner_both)]
    *state, token = run(EARLY, arrays=[far_away(fields), *both])
    far_block = pack_far(fields, outer_both, inner_both, token)
    far = passed(far_block, -2)
    size = rows // PIECES
    edges = pack(
        "pack_edge",
        [close(near), close(token)],
        [(3, size, reach, depth)] * PIECES,
        [(0, i, (i * size, size), ends, (0, size, 0, reach), "inner") for i in range(PIECES)],
    )
    inner_near = [close(passed(piece, 0, inner_pairs)) for piece in edges]
    *state, _ = run(
        MIDDLE, arrays=[close(near), far_away(melt_planes), *both, close(outer_near), *inner_near], state=state
    )
    return run(LATE, arrays=[close(far), far_away(melt_planes), *both], state=state)[0]


def solution(mesh):
    return jax.shard_map(
        body,
        mesh=mesh,
        in_specs=(P(None, "grow", "wide", None), P(None, None, "wide", None), P()),
        out_specs=P(None, "grow", "wide", None),
        check_vma=False,
    )
```

```python
import functools

import jax
import jax.numpy as jnp
from jax import lax
from jax.experimental import pallas as pl
from jax.experimental.pallas import tpu as pltpu
from jax.sharding import PartitionSpec as P

TILE = 8
EARLY, MIDDLE, LATE = 0, 1, 2
EARLY_GROUP = 6
LATE_GROUPS = (8, 6, 4, 2)
PIECES = 2
MIDDLE_FLOPS = 3_500_000_000

coef_phase = 0.15
coef_react = 0.3
coef_couple = 0.4
coef_solute = 1.5
coef_diff = 0.1
coef_heat = 0.16


def passed(value, grow_step, wide_pairs=None):
    grow, wide = lax.axis_size("grow"), lax.axis_size("wide")
    if wide_pairs is None:
        return lax.ppermute(value, "grow", [(g, g + grow_step) for g in range(grow) if 0 <= g + grow_step < grow])
    lanes = wide_pairs + [(b, a) for a, b in wide_pairs]
    if grow_step == 0:
        return lax.ppermute(value, "wide", lanes)
    pairs = [
        (g * wide + a, (g + grow_step) * wide + b)
        for g in range(grow)
        if 0 <= g + grow_step < grow
        for a, b in lanes
    ]
    return lax.ppermute(value, ("grow", "wide"), pairs)


def stage_kernel(stage, rows, cols, slide_rows, *refs):
    *refs, slide_ref = refs
    steps = slide_ref.shape[0]
    reach = steps
    count = rows + 2 * reach
    zero_slot = count + 2 * reach
    first_col = 2 * TILE
    first_row = first_col - reach
    tiles = cols // TILE + 2 * (reach // TILE)
    total_rows = rows * lax.axis_size("grow")
    grow_index, wide_index = lax.axis_index("grow"), lax.axis_index("wide")
    at_end = grow_index == lax.axis_size("grow") - 1
    next_end = grow_index == lax.axis_size("grow") - 2
    is_even = lax.rem(wide_index, 2) == 0
    low_inside = wide_index > 0
    high_inside = wide_index < lax.axis_size("wide") - 1

    slides = slide_rows[...]
    total = jnp.int32(0)
    for k in range(steps):
        shift = slides[k, 0]
        slide_ref[k] = shift
        total = total + shift
    extra = total - reach
    base = grow_index * rows + extra - reach
    low_col, high_col = first_row, first_col + cols
    outer_col = pl.multiple_of(jnp.where(is_even, low_col, high_col), TILE)
    inner_col = pl.multiple_of(jnp.where(is_even, high_col, low_col), TILE)

    if stage == EARLY:
        own, outer_both, inner_both, even, odd, token, sems = refs
    elif stage == MIDDLE:
        near, melt, outer_both, inner_both, outer_near, *inner_near, _, _, even, odd, token, sems = refs
    else:
        far, melt, outer_both, inner_both, _, _, out, even, odd, sems = refs

    def fetch(source, start, col_from, width, length, first, col, sem):
        return pltpu.make_async_copy(
            source.at[:, pl.ds(start, length), pl.ds(col_from, width)],
            even.at[:, pl.ds(reach - extra + first, length), pl.ds(col, width)],
            sems.at[sem],
        )

    def part(first, length, block, outer, inner, sem):
        return [
            fetch(block[0], block[1], block[2], cols, length, first, first_col, sem),
            fetch(outer[0], outer[1], outer[2], reach, length, first, outer_col, sem + 1),
            fetch(inner[0], inner[1], inner[2], reach, length, first, inner_col, sem + 2),
        ]

    def move(source, start, col_from, width, length, first, col):
        def one(i, carry):
            for f in range(3):
                even[f, reach - extra + first + i, pl.ds(col, width)] = source[f, start + i, pl.ds(col_from, width)]
            return carry

        lax.fori_loop(0, length, one, 0, unroll=4)

    def moves():
        if stage == MIDDLE:
            size = rows // PIECES
            move(near, 0, 0, cols, rows, rows, first_col)
            move(outer_near, 0, 0, reach, rows, rows, outer_col)
            for i, piece in enumerate(inner_near):
                move(piece, 0, 0, reach, size, rows + i * size, inner_col)
        elif stage == LATE:
            move(far, 0, 0, cols, reach, 2 * rows, first_col)
            slot = reach - extra + 2 * rows
            for side, (col, low_side) in enumerate(((outer_col, is_even), (inner_col, jnp.logical_not(is_even)))):
                for q in range(reach // 2):
                    for f in range(3):
                        packed = far[f, reach + side, pl.ds(q * reach, reach)]
                        even[f, slot + q, pl.ds(col, reach)] = packed
                        even[f, slot + reach - 1 - q, pl.ds(col, reach)] = turned(packed, q, jnp.logical_not(low_side))

    plain, chosen, special = [], [], None
    if stage == EARLY:
        plain = part(0, rows, (own, 0, 0), (outer_both, 0, 0), (inner_both, 0, 0), 0)
    elif stage == MIDDLE:
        chosen = part(rows, rows, (melt, 0, 0), (outer_both, rows, 0), (inner_both, rows, 0), 0)
        special = at_end
    else:
        chosen = part(2 * rows, reach, (melt, 0, 0), (outer_both, rows, 0), (inner_both, rows, 0), 0)
        special = next_end

    def each(act):
        for copy in plain:
            act(copy)
        if special is None:
            return

        @pl.when(special)
        def _():
            for copy in chosen:
                act(copy)

    each(lambda copy: copy.start())
    if stage != LATE:
        token[...] = jnp.zeros_like(token)
    if stage == EARLY:
        for field in range(3):
            for buffer in (even, odd):
                buffer[field, zero_slot] = jnp.zeros_like(buffer[field, zero_slot])
    if stage == LATE:
        half = rows // 2
        first_half = pltpu.make_async_copy(
            even.at[:, pl.ds(2 * reach, half), pl.ds(first_col, cols)], out.at[:, pl.ds(0, half)], sems.at[3]
        )
        first_half.start()
        single = [
            pltpu.make_async_copy(
                even.at[:, pl.ds(2 * reach + p, 1), pl.ds(first_col, cols)], out.at[:, pl.ds(p, 1)], sems.at[8 + p - half]
            )
            for p in range(half, rows)
        ]
        for p, copy in enumerate(single):
            pl.when(p < rows - half - extra)(copy.start)

    if special is not None:
        pl.when(jnp.logical_not(special))(moves)
    each(lambda copy: copy.wait())

    first_missing = reach - extra + rows
    second_missing = reach - extra + 2 * rows

    def substep(k, source, target, cursor, trim, group):
        next_cursor = cursor + slide_ref[k]
        top = cursor + total_rows - base
        bottom = next_cursor - base
        if stage == EARLY:
            low, high = reach + k + 1, first_missing - 1 - k
        elif stage == MIDDLE:
            low, high = jnp.maximum(first_missing - 1 - k, reach + k + 1), second_missing - 1 - k
        else:
            low, high = second_missing - 1 - k, reach + count - 1 - k

        def advance(j, carry):
            cut = half_tile if stage == LATE and group <= half_tile else trim
            rows_in = (tiles * TILE - 2 * cut) // TILE
            r = low if stage == LATE else high - group * (j + 1)
            slots = [r - 1, r] + [jnp.where(r + q < top, r + q, zero_slot) for q in range(1, group + 1)]
            for t in range(rows_in):
                s0 = first_row + cut + TILE * t
                centre = [[source[f, slot, pl.ds(s0, TILE)] for slot in slots] for f in range(3)]
                for i in range(group):
                    slot = slots[1 + i]
                    value, around = [], []
                    for f in range(3):
                        c = centre[f][1 + i]
                        around.append(
                            (centre[f][i] + centre[f][i + 2])
                            + (source[f, slot, pl.ds(s0 - 1, TILE)] + source[f, slot, pl.ds(s0 + 1, TILE)])
                            + (pltpu.roll(c, 1, 1) + pltpu.roll(c, c.shape[1] - 1, 1))
                        )
                        value.append(c)
                    phase, solute, heat = value
                    squared = phase * phase
                    rest = 1.0 - squared
                    drive = (
                        coef_phase * around[0]
                        + phase * ((1.0 - 6.0 * coef_phase + coef_react) - coef_react * squared)
                        - (rest * rest) * (coef_couple * heat + (coef_couple * coef_solute) * solute)
                    )
                    grown = jnp.tanh(drive)
                    change = 0.5 * (grown - phase)
                    result = [
                        grown,
                        (1.0 - 6.0 * coef_diff) * solute + (coef_diff * around[1] + change),
                        (1.0 - 6.0 * coef_heat) * heat + (coef_heat * around[2] + change),
                    ]
                    if t == 0 and cut < TILE:
                        result = [jnp.where(keep_low[cut], v, 0.0) for v in result]
                    if t == rows_in - 1 and cut < TILE:
                        result = [jnp.where(keep_high[cut], v, 0.0) for v in result]
                    for f in range(3):
                        target[f, r + i, pl.ds(s0, TILE)] = result[f]
            return carry

        if stage == EARLY:
            lax.fori_loop(0, jnp.maximum(high - low + group - 1, 0) // group, advance, 0)
        else:
            advance(0, 0)

        span = pl.ds(first_row, TILE * tiles)

        def clear(r, carry):
            for f in range(3):
                target[f, r, span] = jnp.zeros_like(target[f, r, span])
            return carry

        def keep(r, carry):
            for f in range(3):
                target[f, r, span] = source[f, r, span]
            return carry

        high = jnp.maximum(high, low)

        @pl.when((bottom > low) | (top < high))
        def _():
            lax.fori_loop(low, jnp.clip(bottom, low, high), clear, 0)
            lax.fori_loop(jnp.clip(top, low, high), high, keep, 0)

        return next_cursor

    row = lax.broadcasted_iota(jnp.int32, (TILE, even.shape[3]), 0)
    half_tile = TILE // 2
    keep_low = {0: low_inside, half_tile: low_inside | (row >= half_tile), TILE: True}
    keep_high = {0: high_inside, half_tile: high_inside | (row < half_tile), TILE: True}

    def advance_all(group):
        def pair(trim):
            def run(j, cursor):
                return substep(2 * j + 1, odd, even, substep(2 * j, even, odd, cursor, trim, group), trim, group)

            return run

        wide_pairs = (steps - half_tile) // 2
        cursor = lax.fori_loop(0, wide_pairs, pair(0), jnp.int32(0))
        lax.fori_loop(wide_pairs, steps // 2, pair(half_tile), cursor)

    if stage == EARLY:
        advance_all(EARLY_GROUP)
    elif stage == MIDDLE:
        cursor = jnp.int32(0)
        for k in range(steps):
            buffers = (even, odd) if k % 2 == 0 else (odd, even)
            cursor = substep(k, *buffers, cursor, (k + 1) // half_tile * half_tile, rows)
    else:
        for group, smaller in zip(LATE_GROUPS, LATE_GROUPS[1:] + (0,)):
            pl.when((extra > smaller) & (extra <= group))(functools.partial(advance_all, group))

    if stage == LATE:
        for p, copy in enumerate(single):
            pl.when(p >= rows - half - extra)(copy.start)
        first_half.wait()
        for copy in single:
            copy.wait()


def pack_kernel(plan, *refs):
    sources, targets, sems = refs[: plan[0]], refs[plan[0] : -1], refs[-1]
    wide_index = lax.axis_index("wide")
    copies = []
    for i, (source, target, planes, cols, into, side) in enumerate(plan[1]):
        start, width = cols
        if side is not None:
            first, last = (start, width) if side == "inner" else (width, start)
            start = pl.multiple_of(jnp.where(lax.rem(wide_index, 2) == 0, last, first), TILE)
            width = into[3]
        copies.append(
            pltpu.make_async_copy(
                sources[source].at[:, pl.ds(*planes), pl.ds(start, width)],
                targets[target].at[:, pl.ds(into[0], into[1]), pl.ds(into[2], into[3])],
                sems.at[i],
            )
        )
    for copy in copies:
        copy.start()
    for copy in copies:
        copy.wait()


def turned(rows, count, down):
    if count == 0:
        return rows
    return jnp.where(down, pltpu.roll(rows, count, 0), pltpu.roll(rows, rows.shape[0] - count, 0))


def pack_far_kernel(fields, outer, inner, _, block, sem):
    reach, cols = outer.shape[2], fields.shape[2]
    copy = pltpu.make_async_copy(fields.at[:, pl.ds(0, reach)], block.at[:, pl.ds(0, reach)], sem)
    copy.start()
    is_even = lax.rem(lax.axis_index("wide"), 2) == 0
    row = lax.broadcasted_iota(jnp.int32, (reach, fields.shape[3]), 0)
    for side, (strip, low_side) in enumerate(((outer, is_even), (inner, jnp.logical_not(is_even)))):
        for q in range(cols // reach):
            if q >= reach // 2:
                block[:, reach + side, pl.ds(q * reach, reach)] = jnp.zeros((3, reach, fields.shape[3]), jnp.float32)
                continue
            near_rows = (low_side & (row > q)) | (jnp.logical_not(low_side) & (row < reach - 1 - q))
            for f in range(3):
                second = turned(strip[f, reach - 1 - q], q, low_side)
                block[f, reach + side, pl.ds(q * reach, reach)] = jnp.where(near_rows, strip[f, q], second)
    copy.wait()


def pack_far(fields, outer, inner, token):
    reach, (_, _, cols, depth) = outer.shape[2], fields.shape
    operands, specs = place([(fields, pltpu.HBM), (outer, pltpu.VMEM), (inner, pltpu.VMEM), (token, pltpu.VMEM)])
    return pl.pallas_call(
        pack_far_kernel,
        out_shape=pltpu.VMEM((3, reach + 2, cols, depth), jnp.float32),
        in_specs=specs,
        out_specs=pl.BlockSpec(memory_space=pltpu.VMEM),
        scratch_shapes=[pltpu.SemaphoreType.DMA],
        cost_estimate=pl.CostEstimate(flops=0, bytes_accessed=1000, transcendentals=0),
        compiler_params=pltpu.CompilerParams(vmem_limit_bytes=4 * 1024 * 1024),
        name="pack_far",
    )(*operands)


def place(arrays):
    sources, specs = [], []
    for array, space in arrays:
        sources.append(pltpu.with_memory_space_constraint(array, space))
        specs.append(pl.BlockSpec(memory_space=space))
    return sources, specs


def pack(name, sources, shapes, moves, cost=1000):
    sources, specs = place(sources)
    return pl.pallas_call(
        functools.partial(pack_kernel, (len(sources), moves)),
        out_shape=[pltpu.VMEM(shape, jnp.float32) for shape in shapes],
        in_specs=specs,
        out_specs=[pl.BlockSpec(memory_space=pltpu.VMEM)] * len(shapes),
        scratch_shapes=[pltpu.SemaphoreType.DMA((len(moves),))],
        cost_estimate=pl.CostEstimate(flops=0, bytes_accessed=cost, transcendentals=0),
        compiler_params=pltpu.CompilerParams(vmem_limit_bytes=4 * 1024 * 1024),
        name=name,
    )(*sources)


def run_stage(stage, shape, slide_rows, arrays, state=()):
    _, rows, cols, depth = shape
    reach = slide_rows.shape[0]
    anywhere = pl.BlockSpec(memory_space=pl.ANY)
    in_vmem = pl.BlockSpec(memory_space=pltpu.VMEM)
    held = pltpu.VMEM((3, rows + 4 * reach + 1, cols + 4 * TILE, depth), jnp.float32)
    operands, in_specs = place([(slide_rows, pltpu.VMEM)] + arrays + [(s, pltpu.VMEM) for s in state])
    out_shape, out_specs = [held, held], [in_vmem, in_vmem]
    if stage != LATE:
        out_shape, out_specs = [held, held, pltpu.VMEM((TILE, depth), jnp.float32)], [in_vmem] * 3
    if stage == LATE:
        out_shape, out_specs = [jax.ShapeDtypeStruct(shape, jnp.float32)] + out_shape, [anywhere] + out_specs
    offset = 1 if stage == LATE else 0
    aliases = {len(operands) - 2 + i: offset + i for i in range(2)} if state else {}
    return pl.pallas_call(
        functools.partial(stage_kernel, stage, rows, cols),
        out_shape=out_shape,
        in_specs=in_specs,
        out_specs=out_specs,
        input_output_aliases=aliases,
        scratch_shapes=[pltpu.SemaphoreType.DMA((8 + max(PIECES, rows // 2),)), pltpu.SMEM((reach,), jnp.int32)],
        cost_estimate=pl.CostEstimate(flops=MIDDLE_FLOPS if stage == MIDDLE else 0, bytes_accessed=1000, transcendentals=0),
        compiler_params=pltpu.CompilerParams(vmem_limit_bytes=16 * 1024 * 1024),
        name=("early", "middle", "late")[stage],
    )(*operands)


def body(fields, melt_planes, slide_planes):
    rows, cols, depth = fields.shape[1:]
    reach = slide_planes.shape[0]
    split = rows // 2
    wide = lax.axis_size("wide")
    inner_pairs = [(a, a + 1) for a in range(0, wide - 1, 2)]
    outer_pairs = [(a, a + 1) for a in range(1, wide - 1, 2)]
    is_even = lax.rem(lax.axis_index("wide"), 2) == 0
    inner_start = jnp.where(is_even, cols - reach, 0)

    def edge(block):
        return lax.dynamic_slice_in_dim(block, inner_start, reach, 2)

    def far_away(array):
        return (array, pltpu.HBM)

    def close(array):
        return (array, pltpu.VMEM)

    ends = (0, cols - reach)
    near = passed(fields, -1)
    outer_own, outer_pair, inner_pair = pack(
        "pack_strips",
        [far_away(fields), far_away(melt_planes)],
        [(3, rows, reach, depth), (3, 2 * rows, reach, depth), (3, 2 * rows, reach, depth)],
        [
            (0, 0, (0, rows), ends, (0, rows, 0, reach), "outer"),
            (0, 1, (0, rows), ends, (0, rows, 0, reach), "outer"),
            (1, 1, (0, rows), ends, (rows, rows, 0, reach), "outer"),
            (0, 2, (0, rows), ends, (0, rows, 0, reach), "inner"),
            (1, 2, (0, rows), ends, (rows, rows, 0, reach), "inner"),
        ],
    )
    outer_near = passed(outer_own, -1, outer_pairs)
    outer_both = passed(outer_pair, 0, outer_pairs)
    inner_both = passed(inner_pair, 0, inner_pairs)
    slide_rows = jnp.broadcast_to(slide_planes[:, None], (reach, depth))
    run = functools.partial(run_stage, shape=fields.shape, slide_rows=slide_rows)
    both = [close(outer_both), close(inner_both)]
    *state, token = run(EARLY, arrays=[far_away(fields), *both])
    far_block = pack_far(fields, outer_both, inner_both, token)
    far = passed(far_block, -2)
    size = rows // PIECES
    edges = pack(
        "pack_edge",
        [close(near), close(token)],
        [(3, size, reach, depth)] * PIECES,
        [(0, i, (i * size, size), ends, (0, size, 0, reach), "inner") for i in range(PIECES)],
    )
    inner_near = [close(passed(piece, 0, inner_pairs)) for piece in edges]
    *state, _ = run(
        MIDDLE, arrays=[close(near), far_away(melt_planes), *both, close(outer_near), *inner_near], state=state
    )
    return run(LATE, arrays=[close(far), far_away(melt_planes), *both], state=state)[0]


def solution(mesh):
    return jax.shard_map(
        body,
        mesh=mesh,
        in_specs=(P(None, "grow", "wide", None), P(None, None, "wide", None), P()),
        out_specs=P(None, "grow", "wide", None),
        check_vma=False,
    )
```

```python
import functools

import jax
import jax.numpy as jnp
from jax import lax
from jax.experimental import pallas as pl
from jax.experimental.pallas import tpu as pltpu
from jax.sharding import PartitionSpec as P

TILE = 8
EARLY, MIDDLE, LATE = 0, 1, 2
EARLY_GROUP = 6
LATE_GROUPS = (8, 7, 6, 5, 4, 3, 2, 1)
PIECES = 2
MIDDLE_FLOPS = 3_500_000_000

coef_phase = 0.15
coef_react = 0.3
coef_couple = 0.4
coef_solute = 1.5
coef_diff = 0.1
coef_heat = 0.16


def passed(value, grow_step, wide_pairs=None):
    grow, wide = lax.axis_size("grow"), lax.axis_size("wide")
    if wide_pairs is None:
        return lax.ppermute(value, "grow", [(g, g + grow_step) for g in range(grow) if 0 <= g + grow_step < grow])
    lanes = wide_pairs + [(b, a) for a, b in wide_pairs]
    if grow_step == 0:
        return lax.ppermute(value, "wide", lanes)
    pairs = [
        (g * wide + a, (g + grow_step) * wide + b)
        for g in range(grow)
        if 0 <= g + grow_step < grow
        for a, b in lanes
    ]
    return lax.ppermute(value, ("grow", "wide"), pairs)


def stage_kernel(stage, rows, cols, slide_rows, *refs):
    *refs, slide_ref = refs
    steps = slide_ref.shape[0]
    reach = steps
    count = rows + 2 * reach
    zero_slot = count + 2 * reach
    first_col = 2 * TILE
    first_row = first_col - reach
    tiles = cols // TILE + 2 * (reach // TILE)
    total_rows = rows * lax.axis_size("grow")
    grow_index, wide_index = lax.axis_index("grow"), lax.axis_index("wide")
    at_end = grow_index == lax.axis_size("grow") - 1
    next_end = grow_index == lax.axis_size("grow") - 2
    is_even = lax.rem(wide_index, 2) == 0
    low_inside = wide_index > 0
    high_inside = wide_index < lax.axis_size("wide") - 1

    slides = slide_rows[...]
    total = jnp.int32(0)
    for k in range(steps):
        shift = slides[k, 0]
        slide_ref[k] = shift
        total = total + shift
    extra = total - reach
    base = grow_index * rows + extra - reach
    low_col, high_col = first_row, first_col + cols
    outer_col = pl.multiple_of(jnp.where(is_even, low_col, high_col), TILE)
    inner_col = pl.multiple_of(jnp.where(is_even, high_col, low_col), TILE)

    if stage == EARLY:
        own, outer_both, inner_both, even, odd, token, sems = refs
    elif stage == MIDDLE:
        near, melt, outer_both, inner_both, outer_near, *inner_near, _, _, even, odd, token, sems = refs
    else:
        far, melt, outer_both, inner_both, _, _, out, even, odd, sems = refs

    def fetch(source, start, col_from, width, length, first, col, sem):
        return pltpu.make_async_copy(
            source.at[:, pl.ds(start, length), pl.ds(col_from, width)],
            even.at[:, pl.ds(reach - extra + first, length), pl.ds(col, width)],
            sems.at[sem],
        )

    def part(first, length, block, outer, inner, sem):
        return [
            fetch(block[0], block[1], block[2], cols, length, first, first_col, sem),
            fetch(outer[0], outer[1], outer[2], reach, length, first, outer_col, sem + 1),
            fetch(inner[0], inner[1], inner[2], reach, length, first, inner_col, sem + 2),
        ]

    def move(source, start, col_from, width, length, first, col):
        def one(i, carry):
            for f in range(3):
                even[f, reach - extra + first + i, pl.ds(col, width)] = source[f, start + i, pl.ds(col_from, width)]
            return carry

        lax.fori_loop(0, length, one, 0, unroll=4)

    def moves():
        if stage == MIDDLE:
            size = rows // PIECES
            move(near, 0, 0, cols, rows, rows, first_col)
            move(outer_near, 0, 0, reach, rows, rows, outer_col)
            for i, piece in enumerate(inner_near):
                move(piece, 0, 0, reach, size, rows + i * size, inner_col)
        elif stage == LATE:
            move(far, 0, 0, cols, reach, 2 * rows, first_col)
            slot = reach - extra + 2 * rows
            for side, (col, low_side) in enumerate(((outer_col, is_even), (inner_col, jnp.logical_not(is_even)))):
                for q in range(reach // 2):
                    for f in range(3):
                        packed = far[f, reach + side, pl.ds(q * reach, reach)]
                        even[f, slot + q, pl.ds(col, reach)] = packed
                        even[f, slot + reach - 1 - q, pl.ds(col, reach)] = turned(packed, q, jnp.logical_not(low_side))

    plain, chosen, special = [], [], None
    if stage == EARLY:
        plain = part(0, rows, (own, 0, 0), (outer_both, 0, 0), (inner_both, 0, 0), 0)
    elif stage == MIDDLE:
        chosen = part(rows, rows, (melt, 0, 0), (outer_both, rows, 0), (inner_both, rows, 0), 0)
        special = at_end
    else:
        chosen = part(2 * rows, reach, (melt, 0, 0), (outer_both, rows, 0), (inner_both, rows, 0), 0)
        special = next_end

    def each(act):
        for copy in plain:
            act(copy)
        if special is None:
            return

        @pl.when(special)
        def _():
            for copy in chosen:
                act(copy)

    each(lambda copy: copy.start())
    if stage != LATE:
        token[...] = jnp.zeros_like(token)
    if stage == EARLY:
        for field in range(3):
            for buffer in (even, odd):
                buffer[field, zero_slot] = jnp.zeros_like(buffer[field, zero_slot])
    if stage == LATE:
        half = rows // 2
        first_half = pltpu.make_async_copy(
            even.at[:, pl.ds(2 * reach, half), pl.ds(first_col, cols)], out.at[:, pl.ds(0, half)], sems.at[3]
        )
        first_half.start()
        single = [
            pltpu.make_async_copy(
                even.at[:, pl.ds(2 * reach + p, 1), pl.ds(first_col, cols)], out.at[:, pl.ds(p, 1)], sems.at[8 + p - half]
            )
            for p in range(half, rows)
        ]
        for p, copy in enumerate(single):
            pl.when(p < rows - half - extra)(copy.start)

    if special is not None:
        pl.when(jnp.logical_not(special))(moves)
    each(lambda copy: copy.wait())

    first_missing = reach - extra + rows
    second_missing = reach - extra + 2 * rows

    def substep(k, source, target, cursor, trim, group):
        next_cursor = cursor + slide_ref[k]
        top = cursor + total_rows - base
        bottom = next_cursor - base
        if stage == EARLY:
            low, high = reach + k + 1, first_missing - 1 - k
        elif stage == MIDDLE:
            low, high = jnp.maximum(first_missing - 1 - k, reach + k + 1), second_missing - 1 - k
        else:
            low, high = second_missing - 1 - k, reach + count - 1 - k

        def advance(j, carry):
            cut = half_tile if stage == LATE and group <= half_tile + 1 else trim
            rows_in = (tiles * TILE - 2 * cut) // TILE
            r = low if stage == LATE else high - group * (j + 1)
            slots = [r - 1, r] + [jnp.where(r + q < top, r + q, zero_slot) for q in range(1, group + 1)]
            for t in range(rows_in):
                s0 = first_row + cut + TILE * t
                centre = [[source[f, slot, pl.ds(s0, TILE)] for slot in slots] for f in range(3)]
                for i in range(group):
                    slot = slots[1 + i]
                    value, around = [], []
                    for f in range(3):
                        c = centre[f][1 + i]
                        around.append(
                            (centre[f][i] + centre[f][i + 2])
                            + (source[f, slot, pl.ds(s0 - 1, TILE)] + source[f, slot, pl.ds(s0 + 1, TILE)])
                            + (pltpu.roll(c, 1, 1) + pltpu.roll(c, c.shape[1] - 1, 1))
                        )
                        value.append(c)
                    phase, solute, heat = value
                    squared = phase * phase
                    rest = 1.0 - squared
                    drive = (
                        coef_phase * around[0]
                        + phase * ((1.0 - 6.0 * coef_phase + coef_react) - coef_react * squared)
                        - (rest * rest) * (coef_couple * heat + (coef_couple * coef_solute) * solute)
                    )
                    grown = jnp.tanh(drive)
                    change = 0.5 * (grown - phase)
                    result = [
                        grown,
                        (1.0 - 6.0 * coef_diff) * solute + (coef_diff * around[1] + change),
                        (1.0 - 6.0 * coef_heat) * heat + (coef_heat * around[2] + change),
                    ]
                    if t == 0 and cut < TILE:
                        result = [jnp.where(keep_low[cut], v, 0.0) for v in result]
                    if t == rows_in - 1 and cut < TILE:
                        result = [jnp.where(keep_high[cut], v, 0.0) for v in result]
                    for f in range(3):
                        target[f, r + i, pl.ds(s0, TILE)] = result[f]
            return carry

        if stage == EARLY:
            lax.fori_loop(0, jnp.maximum(high - low + group - 1, 0) // group, advance, 0)
        else:
            advance(0, 0)

        span = pl.ds(first_row, TILE * tiles)

        def clear(r, carry):
            for f in range(3):
                target[f, r, span] = jnp.zeros_like(target[f, r, span])
            return carry

        def keep(r, carry):
            for f in range(3):
                target[f, r, span] = source[f, r, span]
            return carry

        high = jnp.maximum(high, low)

        @pl.when((bottom > low) | (top < high))
        def _():
            lax.fori_loop(low, jnp.clip(bottom, low, high), clear, 0)
            lax.fori_loop(jnp.clip(top, low, high), high, keep, 0)

        return next_cursor

    row = lax.broadcasted_iota(jnp.int32, (TILE, even.shape[3]), 0)
    half_tile = TILE // 2
    keep_low = {0: low_inside, half_tile: low_inside | (row >= half_tile), TILE: True}
    keep_high = {0: high_inside, half_tile: high_inside | (row < half_tile), TILE: True}

    def advance_all(group):
        def pair(trim):
            def run(j, cursor):
                return substep(2 * j + 1, odd, even, substep(2 * j, even, odd, cursor, trim, group), trim, group)

            return run

        wide_pairs = (steps - half_tile) // 2
        cursor = lax.fori_loop(0, wide_pairs, pair(0), jnp.int32(0))
        lax.fori_loop(wide_pairs, steps // 2, pair(half_tile), cursor)

    if stage == EARLY:
        advance_all(EARLY_GROUP)
    elif stage == MIDDLE:
        cursor = jnp.int32(0)
        for k in range(steps):
            buffers = (even, odd) if k % 2 == 0 else (odd, even)
            cursor = substep(k, *buffers, cursor, (k + 1) // half_tile * half_tile, rows)
    else:
        for group, smaller in zip(LATE_GROUPS, LATE_GROUPS[1:] + (0,)):
            pl.when((extra > smaller) & (extra <= group))(functools.partial(advance_all, group))

    if stage == LATE:
        for p, copy in enumerate(single):
            pl.when(p >= rows - half - extra)(copy.start)
        first_half.wait()
        for copy in single:
            copy.wait()


def pack_kernel(plan, *refs):
    sources, targets, sems = refs[: plan[0]], refs[plan[0] : -1], refs[-1]
    wide_index = lax.axis_index("wide")
    copies = []
    for i, (source, target, planes, cols, into, side) in enumerate(plan[1]):
        start, width = cols
        if side is not None:
            first, last = (start, width) if side == "inner" else (width, start)
            start = pl.multiple_of(jnp.where(lax.rem(wide_index, 2) == 0, last, first), TILE)
            width = into[3]
        copies.append(
            pltpu.make_async_copy(
                sources[source].at[:, pl.ds(*planes), pl.ds(start, width)],
                targets[target].at[:, pl.ds(into[0], into[1]), pl.ds(into[2], into[3])],
                sems.at[i],
            )
        )
    for copy in copies:
        copy.start()
    for copy in copies:
        copy.wait()


def turned(rows, count, down):
    if count == 0:
        return rows
    return jnp.where(down, pltpu.roll(rows, count, 0), pltpu.roll(rows, rows.shape[0] - count, 0))


def pack_far_kernel(fields, outer, inner, _, block, sem):
    reach, cols = outer.shape[2], fields.shape[2]
    copy = pltpu.make_async_copy(fields.at[:, pl.ds(0, reach)], block.at[:, pl.ds(0, reach)], sem)
    copy.start()
    is_even = lax.rem(lax.axis_index("wide"), 2) == 0
    row = lax.broadcasted_iota(jnp.int32, (reach, fields.shape[3]), 0)
    for side, (strip, low_side) in enumerate(((outer, is_even), (inner, jnp.logical_not(is_even)))):
        for q in range(cols // reach):
            if q >= reach // 2:
                block[:, reach + side, pl.ds(q * reach, reach)] = jnp.zeros((3, reach, fields.shape[3]), jnp.float32)
                continue
            near_rows = (low_side & (row > q)) | (jnp.logical_not(low_side) & (row < reach - 1 - q))
            for f in range(3):
                second = turned(strip[f, reach - 1 - q], q, low_side)
                block[f, reach + side, pl.ds(q * reach, reach)] = jnp.where(near_rows, strip[f, q], second)
    copy.wait()


def pack_far(fields, outer, inner, token):
    reach, (_, _, cols, depth) = outer.shape[2], fields.shape
    operands, specs = place([(fields, pltpu.HBM), (outer, pltpu.VMEM), (inner, pltpu.VMEM), (token, pltpu.VMEM)])
    return pl.pallas_call(
        pack_far_kernel,
        out_shape=pltpu.VMEM((3, reach + 2, cols, depth), jnp.float32),
        in_specs=specs,
        out_specs=pl.BlockSpec(memory_space=pltpu.VMEM),
        scratch_shapes=[pltpu.SemaphoreType.DMA],
        cost_estimate=pl.CostEstimate(flops=0, bytes_accessed=1000, transcendentals=0),
        compiler_params=pltpu.CompilerParams(vmem_limit_bytes=4 * 1024 * 1024),
        name="pack_far",
    )(*operands)


def place(arrays):
    sources, specs = [], []
    for array, space in arrays:
        sources.append(pltpu.with_memory_space_constraint(array, space))
        specs.append(pl.BlockSpec(memory_space=space))
    return sources, specs


def pack(name, sources, shapes, moves, cost=1000):
    sources, specs = place(sources)
    return pl.pallas_call(
        functools.partial(pack_kernel, (len(sources), moves)),
        out_shape=[pltpu.VMEM(shape, jnp.float32) for shape in shapes],
        in_specs=specs,
        out_specs=[pl.BlockSpec(memory_space=pltpu.VMEM)] * len(shapes),
        scratch_shapes=[pltpu.SemaphoreType.DMA((len(moves),))],
        cost_estimate=pl.CostEstimate(flops=0, bytes_accessed=cost, transcendentals=0),
        compiler_params=pltpu.CompilerParams(vmem_limit_bytes=4 * 1024 * 1024),
        name=name,
    )(*sources)


def run_stage(stage, shape, slide_rows, arrays, state=()):
    _, rows, cols, depth = shape
    reach = slide_rows.shape[0]
    anywhere = pl.BlockSpec(memory_space=pl.ANY)
    in_vmem = pl.BlockSpec(memory_space=pltpu.VMEM)
    held = pltpu.VMEM((3, rows + 4 * reach + 1, cols + 4 * TILE, depth), jnp.float32)
    operands, in_specs = place([(slide_rows, pltpu.VMEM)] + arrays + [(s, pltpu.VMEM) for s in state])
    out_shape, out_specs = [held, held], [in_vmem, in_vmem]
    if stage != LATE:
        out_shape, out_specs = [held, held, pltpu.VMEM((TILE, depth), jnp.float32)], [in_vmem] * 3
    if stage == LATE:
        out_shape, out_specs = [jax.ShapeDtypeStruct(shape, jnp.float32)] + out_shape, [anywhere] + out_specs
    offset = 1 if stage == LATE else 0
    aliases = {len(operands) - 2 + i: offset + i for i in range(2)} if state else {}
    return pl.pallas_call(
        functools.partial(stage_kernel, stage, rows, cols),
        out_shape=out_shape,
        in_specs=in_specs,
        out_specs=out_specs,
        input_output_aliases=aliases,
        scratch_shapes=[pltpu.SemaphoreType.DMA((8 + max(PIECES, rows // 2),)), pltpu.SMEM((reach,), jnp.int32)],
        cost_estimate=pl.CostEstimate(flops=MIDDLE_FLOPS if stage == MIDDLE else 0, bytes_accessed=1000, transcendentals=0),
        compiler_params=pltpu.CompilerParams(vmem_limit_bytes=16 * 1024 * 1024),
        name=("early", "middle", "late")[stage],
    )(*operands)


def body(fields, melt_planes, slide_planes):
    rows, cols, depth = fields.shape[1:]
    reach = slide_planes.shape[0]
    split = rows // 2
    wide = lax.axis_size("wide")
    inner_pairs = [(a, a + 1) for a in range(0, wide - 1, 2)]
    outer_pairs = [(a, a + 1) for a in range(1, wide - 1, 2)]
    is_even = lax.rem(lax.axis_index("wide"), 2) == 0
    inner_start = jnp.where(is_even, cols - reach, 0)

    def edge(block):
        return lax.dynamic_slice_in_dim(block, inner_start, reach, 2)

    def far_away(array):
        return (array, pltpu.HBM)

    def close(array):
        return (array, pltpu.VMEM)

    ends = (0, cols - reach)
    near = passed(fields, -1)
    outer_own, outer_pair, inner_pair = pack(
        "pack_strips",
        [far_away(fields), far_away(melt_planes)],
        [(3, rows, reach, depth), (3, 2 * rows, reach, depth), (3, 2 * rows, reach, depth)],
        [
            (0, 0, (0, rows), ends, (0, rows, 0, reach), "outer"),
            (0, 1, (0, rows), ends, (0, rows, 0, reach), "outer"),
            (1, 1, (0, rows), ends, (rows, rows, 0, reach), "outer"),
            (0, 2, (0, rows), ends, (0, rows, 0, reach), "inner"),
            (1, 2, (0, rows), ends, (rows, rows, 0, reach), "inner"),
        ],
    )
    outer_near = passed(outer_own, -1, outer_pairs)
    outer_both = passed(outer_pair, 0, outer_pairs)
    inner_both = passed(inner_pair, 0, inner_pairs)
    slide_rows = jnp.broadcast_to(slide_planes[:, None], (reach, depth))
    run = functools.partial(run_stage, shape=fields.shape, slide_rows=slide_rows)
    both = [close(outer_both), close(inner_both)]
    *state, token = run(EARLY, arrays=[far_away(fields), *both])
    far_block = pack_far(fields, outer_both, inner_both, token)
    far = passed(far_block, -2)
    size = rows // PIECES
    edges = pack(
        "pack_edge",
        [close(near), close(token)],
        [(3, size, reach, depth)] * PIECES,
        [(0, i, (i * size, size), ends, (0, size, 0, reach), "inner") for i in range(PIECES)],
    )
    inner_near = [close(passed(piece, 0, inner_pairs)) for piece in edges]
    *state, _ = run(
        MIDDLE, arrays=[close(near), far_away(melt_planes), *both, close(outer_near), *inner_near], state=state
    )
    return run(LATE, arrays=[close(far), far_away(melt_planes), *both], state=state)[0]


def solution(mesh):
    return jax.shard_map(
        body,
        mesh=mesh,
        in_specs=(P(None, "grow", "wide", None), P(None, None, "wide", None), P()),
        out_specs=P(None, "grow", "wide", None),
        check_vma=False,
    )
```
